256 devices in a mesh: pipe: 8 (over z_lo, y), dp: 32 (over x, z_hi, core).
Axes of the slice: x: 4, y: 4, z: 8 (z_hi: 4, z_lo: 2; z = z_hi * 2 + z_lo), core: 2. Of those that a mesh axis runs over, the one named last changes fastest.
Arguments:
- queries: bfloat16 [2, 8, 2048, 4096], P(None, 'pipe', 'dp'), may hold values from -5 to 5
- keys: bfloat16 [2, 8, 2048, 512], P(None, 'pipe', 'dp'), may hold values from -5 to 5
- values: bfloat16 [2, 8, 2048, 512], P(None, 'pipe', 'dp'), may hold values from -5 to 5
- out_grad: bfloat16 [2, 8, 2048, 4096], P(None, 'pipe', 'dp'), may hold values from -6 to 6
- block_input: bfloat16 [2, 8, 2048, 8192], P(None, 'pipe', 'dp'), may hold values from -64 to 64
- positions: int32 [2, 8, 2048], P(None, 'pipe', 'dp'), may hold values from 0 to 63, as said below
- direction: int32 [2], replicated, may hold values from 0 to 1, each once
- key_weight: bfloat16 [8, 8192, 512], P('pipe', 'dp'), may hold values from -0.1875 to 0.1875
- value_weight: bfloat16 [8, 8192, 512], P('pipe', 'dp'), may hold values from -0.1875 to 0.1875
- gain: bfloat16 [8, 8192], P('pipe', 'dp'), may hold values from 0.099609375 to 1.8984375
Outputs:
- query_grad: bfloat16 [2, 8, 2048, 4096], P(None, 'pipe', 'dp')
- passed_grad: bfloat16 [2, 8, 2048, 8192], P(None, 'pipe', 'dp')
- key_weight_grad: float32 [8, 8192, 512], P('pipe', 'dp')
- value_weight_grad: float32 [8, 8192, 512], P('pipe', 'dp')
- gain_grad: float32 [8, 8192], P('pipe', 'dp')
The draws below stay inside these ranges and needn't reach their ends.
Inputs may be any that keep to these rules, and one draw needn't show every extreme that they name: `positions`: within every aligned block of 64 tokens the first position is 0, and each later position is the previous one plus 1 or else 0 where a new document starts. `direction`: the two entries are 0 and 1 in some order.
All inputs are finite; a program needn't handle non-finite values.
Results may differ from the reference program's by a relative error of at most 0.025.
Values may be sent and summed in bfloat16 or wider, within the bound.
A program may use at most 128 MiB of HBM per device.

```python
import jax
import jax.numpy as jnp
from jax import lax

D = 8192
KVH = 4
HD = 128
SEQ = 64
GROUP = 8
QW = 4096
KVW = 512
SECTIONS = 8
TOK = 2048
N_DP = 32


def doc_starts(key):
    flags = jax.random.randint(key, (2, SECTIONS, N_DP, SEQ), 0, 32) == 0
    later_rows = (jnp.arange(N_DP, dtype=jnp.int32) != 0)[None, None, :, None]
    flags = jnp.logical_and(flags, later_rows)
    first = jnp.arange(SEQ, dtype=jnp.int32) == 0
    return jnp.logical_or(flags, first[None, None, None, :]).reshape(2, SECTIONS, TOK)


def draw_positions(key, part):
    starts = doc_starts(key)
    token_index = jnp.broadcast_to(jnp.arange(TOK, dtype=jnp.int32), (2, SECTIONS, TOK))
    latest = lax.cummax(jnp.where(starts, token_index, 0), axis=2)
    return (token_index - latest).astype(jnp.int32)


def draw_queries(key, part):
    key = jax.random.fold_in(key, 7)
    result = jnp.clip(jax.random.normal(key, (2, SECTIONS, TOK, QW), jnp.float32), -4.8, 4.8)
    return result.astype(jnp.bfloat16)


def draw_keys(key, part):
    key = jax.random.fold_in(key, 9)
    result = jnp.clip(jax.random.normal(key, (2, SECTIONS, TOK, KVW), jnp.float32), -4.8, 4.8)
    return result.astype(jnp.bfloat16)


def draw_block_input(key, part):
    key = jax.random.fold_in(key, 3)
    first, second, third = jax.random.split(key, 3)
    row_scale = jnp.exp(jax.random.uniform(second, (2, SECTIONS, TOK, 1), jnp.float32, -0.92, 1.39))
    col_scale = jnp.exp(jax.random.uniform(third, (1, 1, 1, D), jnp.float32, -0.92, 1.39))
    drawn = jnp.clip(jax.random.normal(first, (2, SECTIONS, TOK, D), jnp.float32), -4.0, 4.0)
    return (drawn * row_scale * col_scale).astype(jnp.bfloat16)


def block_scale(own_key, shape, cuts, smallest, high):
    def one(position, blocks):
        steps = jax.random.uniform(jax.random.fold_in(jax.random.fold_in(own_key, 6), position), (blocks,), jnp.float32, smallest / len(cuts), high / len(cuts))
        return jnp.repeat(jnp.exp(steps), shape[position] // blocks).reshape((-1,) + (1,) * (len(shape) - position - 1))

    level = one(*cuts[0])
    for cut in cuts[1:]:
        level = level * one(*cut)
    return level


def bell_draw(key, shape, deviation, most, shards=(), held_as=jnp.bfloat16):
    entries = jax.random.normal(key, shape, jnp.float32) * deviation
    if len(shards) > 0:
        entries = block_scale(key, shape, shards, -0.22, 0.18) * entries
    return jnp.clip(entries, min=-most, max=most).astype(held_as)


def setup_inputs(seed: int = 0) -> dict:
    key_list = jax.random.split(jax.random.key(seed), 11)
    queries = draw_queries(jax.random.fold_in(key_list[10], 71), 0)
    keys = draw_keys(jax.random.fold_in(key_list[10], 71), 0)
    values = bell_draw(key_list[2], (2, SECTIONS, TOK, KVW), 1.0, 5.0, ((1, 8), (2, 32)))
    out_grad = bell_draw(key_list[3], (2, SECTIONS, TOK, QW), 1.0, 6.0, ((1, 8), (2, 32)))
    block_input = draw_block_input(jax.random.fold_in(key_list[10], 71), 0)
    positions = draw_positions(jax.random.fold_in(key_list[10], 71), 0)
    direction = jax.random.permutation(key_list[6], 2).astype(jnp.int32)
    key_weight = bell_draw(key_list[7], (SECTIONS, D, KVW), (2 * KVW) ** -0.5, 0.1875, ((0, 8), (1, 32)))
    value_weight = bell_draw(key_list[8], (SECTIONS, D, KVW), (2 * KVW) ** -0.5, 0.1875, ((0, 8), (1, 32)))
    gain = jnp.clip(1.0 + 0.18 * jax.random.normal(key_list[9], (SECTIONS, D), jnp.float32), 0.099609375, 1.8984375).astype(jnp.bfloat16)
    return dict(queries=queries, keys=keys, values=values, out_grad=out_grad, block_input=block_input, positions=positions, direction=direction, key_weight=key_weight, value_weight=value_weight, gain=gain)


def attention_grads(queries, keys, values, out_grad, positions):
    count = queries.shape[0]
    length = queries.shape[1]
    scale = HD ** (-0.5)
    query_heads = queries.astype(jnp.float32).reshape(count, length, KVH, GROUP, HD)
    key_heads = keys.astype(jnp.float32).reshape(count, length, KVH, HD)
    value_heads = values.astype(jnp.float32).reshape(count, length, KVH, HD)
    grad_heads = out_grad.astype(jnp.float32).reshape(count, length, KVH, GROUP, HD)
    scores = jnp.einsum('nqkgd,nskd->nkgqs', query_heads, key_heads) * scale
    token_index = jnp.arange(length, dtype=jnp.int32)
    doc_start = token_index[None, :] - positions
    visible = (token_index[:, None] >= token_index[None, :])[None] & (doc_start[:, :, None] == doc_start[:, None, :])
    scores = jnp.where(visible[:, None, None], scores, -1e+30)
    top = lax.optimization_barrier(jnp.max(scores, axis=-1, keepdims=True))
    weights = jnp.exp(scores - top)
    probs = weights / lax.optimization_barrier(jnp.sum(weights, axis=-1, keepdims=True))
    probs_b = lax.optimization_barrier(probs.astype(jnp.bfloat16)).astype(jnp.float32)
    attn = jnp.einsum('nkgqs,nskd->nqkgd', probs_b, value_heads)
    attn_b = lax.optimization_barrier(attn.astype(jnp.bfloat16)).astype(jnp.float32)
    delta = lax.optimization_barrier(jnp.sum(grad_heads * attn_b, axis=-1))
    delta = jnp.transpose(delta, (0, 2, 3, 1))
    dprobs = jnp.einsum('nqkgd,nskd->nkgqs', grad_heads, value_heads)
    dscore = probs * (dprobs - delta[..., None])
    dscore_b = lax.optimization_barrier(dscore.astype(jnp.bfloat16)).astype(jnp.float32)
    query_grad = (jnp.einsum('nkgqs,nskd->nqkgd', dscore_b, key_heads) * scale).astype(jnp.bfloat16)
    key_grad = (jnp.einsum('nkgqs,nqkgd->nskd', dscore_b, query_heads) * scale).astype(jnp.bfloat16)
    value_grad = jnp.einsum('nkgqs,nqkgd->nskd', probs_b, grad_heads).astype(jnp.bfloat16)
    return (query_grad.reshape(count * length, QW), key_grad.reshape(count * length, KVW), value_grad.reshape(count * length, KVW))

def reference(queries, keys, values, out_grad, block_input, positions, direction, key_weight, value_weight, gain):
    key_total = jnp.zeros((SECTIONS, D, KVW), jnp.float32)
    value_total = jnp.zeros((SECTIONS, D, KVW), jnp.float32)
    gain_total = jnp.zeros((SECTIONS, D), jnp.float32)
    query_rows = []
    passed_rows = []
    for micro in range(2):
        branches = []
        query_list = []
        for section in range(SECTIONS):
            layer = jnp.where(direction[micro] == 0, section, SECTIONS - 1 - section).astype(jnp.int32)
            weights = jnp.concatenate([key_weight[layer], value_weight[layer]], axis=1)
            gains = gain[layer].astype(jnp.float32)
            inputs = block_input[micro, section].astype(jnp.float32)
            inv_rms = lax.rsqrt(lax.optimization_barrier(jnp.mean(inputs * inputs, axis=-1, keepdims=True)) + 1e-05)
            scaled = inputs * inv_rms
            normed = lax.optimization_barrier(scaled.astype(jnp.bfloat16))
            hidden = (normed.astype(jnp.float32) * gains).astype(jnp.bfloat16)
            query_grad, key_grad, value_grad = attention_grads(queries[micro, section].reshape(N_DP, SEQ, QW), keys[micro, section].reshape(N_DP, SEQ, KVW), values[micro, section].reshape(N_DP, SEQ, KVW), out_grad[micro, section].reshape(N_DP, SEQ, QW), positions[micro, section].reshape(N_DP, SEQ))
            query_list.append(query_grad)
            kv_grad = jnp.concatenate([key_grad, value_grad], axis=1)
            hidden_grad = jnp.dot(kv_grad, weights.T, preferred_element_type=jnp.float32)
            weight_grad = jnp.dot(hidden.T, kv_grad, preferred_element_type=jnp.float32)
            key_total = key_total.at[layer].add(weight_grad[:, :KVW])
            value_total = value_total.at[layer].add(weight_grad[:, KVW:])
            gain_total = gain_total.at[layer].add(lax.optimization_barrier(jnp.sum(hidden_grad * normed.astype(jnp.float32), axis=0)))
            normed_grad = lax.optimization_barrier((hidden_grad * gains).astype(jnp.bfloat16)).astype(jnp.float32)
            branch = inv_rms * (normed_grad - scaled * lax.optimization_barrier(jnp.mean(normed_grad * scaled, axis=-1, keepdims=True)))
            branches.append(branch.astype(jnp.bfloat16))
        empty = jnp.zeros((TOK, D), jnp.bfloat16)
        passed_list = []
        for section in range(SECTIONS):
            after = branches[section + 1] if section + 1 < SECTIONS else empty
            before = branches[section - 1] if section > 0 else empty
            passed_list.append(jnp.where(direction[micro] == 0, after, before))
        query_rows.append(jnp.stack(query_list))
        passed_rows.append(jnp.stack(passed_list))
    return (jnp.stack(query_rows), jnp.stack(passed_rows), key_total, value_total, gain_total)
```

```python
import functools

import jax
import jax.numpy as jnp
from jax import lax
from jax.experimental import pallas as pl
from jax.experimental.pallas import tpu as pltpu
from jax.sharding import PartitionSpec as P

KVH = 4
HD = 128
GROUP = 8
SEQ = 64
QW = 4096
KVW = 512
D = 8192
BLK = 256
KW = 2 * KVW
KX = KW + 128
HALF = BLK // 2
MESH = pl.DeviceIdType.MESH
F32 = jnp.float32
BF16 = jnp.bfloat16


def dot(a, b, ca, cb):
    return lax.dot_general(a, b, (((ca,), (cb,)), ((), ())), preferred_element_type=F32)


def kernel(
    flag,
    pos,
    keys,
    values,
    gain,
    q_hbm,
    og_hbm,
    inp_hbm,
    kw_hbm,
    vw_hbm,
    qg_out,
    passed_out,
    wk_out,
    wv_out,
    gg_out,
    q,
    og,
    inp,
    nsend,
    nrecv,
    invs,
    vis,
    kvm,
    kvsnd,
    kvall,
    wall,
    gall,
    hbuf,
    part,
    rsf_s,
    rsf_r,
    rsn_s,
    rsn_r,
    ngb,
    cacc,
    gpart,
    gg_r,
    c_s,
    c_r,
    cbuf,
    bsend,
    brecv,
    lsem,
    ns_s,
    ns_r,
    g_s,
    g_r,
    km_s,
    km_r,
    kx_s,
    kx_r,
    kc_s,
    kc_r,
    w_s,
    w_r,
    rs_s,
    rs_r,
    gg_ss,
    gg_rs,
    c_ss,
    c_rs,
    b_s,
    b_r,
):
    p = lax.axis_index("pipe")
    d = lax.axis_index("dp")
    zl = lax.div(p, 4)
    x = lax.div(d, 8)
    zh = lax.rem(lax.div(d, 2), 4)
    c = lax.rem(d, 2)
    slot = x * 2 + c
    zp = lax.rem(zh + 1, 4)
    zf = lax.rem(zh + 2, 4)
    zm = lax.rem(zh + 3, 4)

    def dev(pp, xx, zz, cc):
        return (pp, xx * 8 + zz * 2 + cc)

    def mir(cc):
        return lax.rem(zh + 4 + cc * (2 * zl - 1), 4)

    def remote(src, dst, ss, rs, to):
        return pltpu.make_async_remote_copy(
            src_ref=src, dst_ref=dst, send_sem=ss, recv_sem=rs, device_id=to, device_id_type=MESH
        )

    def here(ss, rs, ref):
        return remote(ref, ref, ss, rs, dev(p, x, zh, 1 - c))

    def loop(lo, hi, f):
        def step(i, carry):
            f(i)
            return carry

        lax.fori_loop(lo, hi, step, 0)

    load_inp = pltpu.make_async_copy(inp_hbm, inp, lsem.at[0])
    load_kw = pltpu.make_async_copy(kw_hbm, wall.at[zh, :, pl.ds(0, KVW)], lsem.at[1])
    load_vw = pltpu.make_async_copy(vw_hbm, wall.at[zh, :, pl.ds(KVW, KVW)], lsem.at[2])
    load_q = pltpu.make_async_copy(q_hbm, q, lsem.at[3])
    load_og = pltpu.make_async_copy(og_hbm, og, lsem.at[4])
    load_kw.start()
    load_vw.start()
    load_inp.start()
    load_q.start()
    load_og.start()

    bar = pltpu.get_barrier_semaphore()

    def greet(to):
        pl.semaphore_signal(bar, inc=1, device_id=to, device_id_type=MESH)

    back_up = p >= 1
    back_down = p <= 6
    self_up = jnp.logical_and(p == 4, c == 0)
    zlm = lax.div(p + 3, 4) - 1
    zup = lax.rem(zh + 4 + c * (2 * zlm - 1), 4)

    for zz in (zp, zm, zf):
        greet(dev(p, x, zz, c))

    def greet_all(j):
        t = lax.rem(slot + j, 8)
        xx = lax.div(t, 2)
        cc = lax.rem(t, 2)

        @pl.when(j > 0)
        def _():
            greet(dev(p, xx, zh, cc))

        greet(dev(7 - p, xx, mir(cc), cc))

        @pl.when(back_down)
        def _():
            greet(dev(p + 1, xx, zh, cc))

        @pl.when(jnp.logical_and(back_up, jnp.logical_not(jnp.logical_and(self_up, j == 0))))
        def _():
            greet(dev(8 - p, xx, zup, cc))

    loop(0, 8, greet_all)
    gall[zh] = jnp.broadcast_to(gain[...], (16, BLK))
    n_back = jnp.where(back_up, 16, 0) - jnp.where(self_up, 1, 0)
    pl.semaphore_wait(bar, 18 + n_back)

    for j, zz in ((1, zp), (2, zf), (3, zm)):
        remote(gall.at[zh], gall.at[zh], g_s.at[j], g_r.at[j], dev(p, x, zz, c)).start()
    load_kw.wait()
    load_vw.wait()
    remote(wall.at[zh], wall.at[zh], w_s.at[0], w_r.at[0], dev(p, x, zp, c)).start()
    remote(wall.at[zh], wall.at[zh], w_s.at[1], w_r.at[1], dev(p, x, zm, c)).start()

    swap = flag[0] == 1
    load_inp.wait()

    def norm_rows(i):
        r = pl.ds(pl.multiple_of(i * 16, 16), 16)
        sq = [jnp.zeros((16, BLK), F32), jnp.zeros((16, BLK), F32)]
        for j in range(32):
            for m in range(2):
                v = inp[m, r, j * BLK : (j + 1) * BLK].astype(F32)
                sq[m] = sq[m] + v * v
        inv = [lax.rsqrt(jnp.sum(s, axis=1, keepdims=True) * (1.0 / D) + 1e-05) for s in sq]
        for j in range(32):
            t = (j // 8) * 2 + j % 2
            b = (j // 2) % 4
            v0 = inp[0, r, j * BLK : (j + 1) * BLK].astype(F32) * inv[0]
            v1 = inp[1, r, j * BLK : (j + 1) * BLK].astype(F32) * inv[1]
            nsend[0, t, b, r, :] = jnp.where(swap, v1, v0).astype(BF16)
            nsend[1, t, b, r, :] = jnp.where(swap, v0, v1).astype(BF16)
        i0 = jnp.broadcast_to(inv[0], (16, 128))
        i1 = jnp.broadcast_to(inv[1], (16, 128))
        invs[0, r, :] = jnp.where(swap, i1, i0)
        invs[1, r, :] = jnp.where(swap, i0, i1)

    loop(0, SEQ // 16, norm_rows)

    def send_norm(j):
        t = lax.rem(slot + j, 8)
        xx = lax.div(t, 2)
        cc = lax.rem(t, 2)
        remote(
            nsend.at[1, t], nrecv.at[1, slot], ns_s.at[1, t], ns_r.at[1, slot], dev(7 - p, xx, mir(c), cc)
        ).start()

        @pl.when(j > 0)
        def _():
            remote(
                nsend.at[0, t], nrecv.at[0, slot], ns_s.at[0, t], ns_r.at[0, slot], dev(p, xx, zh, cc)
            ).start()

    loop(0, 8, send_norm)
    own_norm = pltpu.make_async_copy(nsend.at[0, slot], nrecv.at[0, slot], lsem.at[5])
    own_norm.start()

    eye64 = lax.broadcasted_iota(jnp.int32, (SEQ, SEQ), 0) == lax.broadcasted_iota(
        jnp.int32, (SEQ, SEQ), 1
    )
    row_id = lax.broadcasted_iota(jnp.int32, (SEQ, SEQ), 0)
    col_id = lax.broadcasted_iota(jnp.int32, (SEQ, SEQ), 1)
    for m in range(2):
        start_row = (col_id - pos[m]).astype(F32)
        start_col = jnp.sum(jnp.where(eye64, start_row, 0.0), axis=1, keepdims=True)
        seen = jnp.logical_and(row_id >= col_id, start_row == start_col)
        vis[m] = jnp.where(seen, 1.0, 0.0)
    load_q.wait()
    load_og.wait()
    scale = HD ** (-0.5)

    def attend(i):
        m = lax.div(i, KVH)
        k = lax.rem(i, KVH)
        cols = pl.ds(pl.multiple_of(k * HD, HD), HD)
        heads = [
            pl.ds(pl.multiple_of(k * (GROUP * HD) + g * HD, HD), HD) for g in range(GROUP)
        ]
        kk = keys[m, :, cols]
        vv = values[m, :, cols]
        qs = jnp.concatenate([q[m, :, h] for h in heads], axis=0)
        gs = jnp.concatenate([og[m, :, h] for h in heads], axis=0)
        seen = jnp.concatenate([vis[m]] * GROUP, axis=0) > 0.5
        s = jnp.where(seen, dot(qs, kk, 1, 1) * scale, -1e30)
        w = jnp.exp(s - jnp.max(s, axis=1, keepdims=True))
        probs = w / jnp.sum(w, axis=1, keepdims=True)
        pb = probs.astype(BF16)
        attn = dot(pb, vv, 1, 0).astype(BF16)
        delta = jnp.sum(gs.astype(F32) * attn.astype(F32), axis=1, keepdims=True)
        ds = (probs * (dot(gs, vv, 1, 1) - delta)).astype(BF16)
        qg = (dot(ds, kk, 1, 0) * scale).astype(BF16)
        for g, h in enumerate(heads):
            qg_out[m, :, h] = qg[g * SEQ : (g + 1) * SEQ]
        kvm[m, :, cols] = (dot(ds, qs, 0, 0) * scale).astype(BF16)
        kvm[m, :, pl.ds(pl.multiple_of(KVW + k * HD, HD), HD)] = dot(pb, gs, 0, 0).astype(BF16)

    loop(0, 2 * KVH, attend)

    lane = lax.broadcasted_iota(jnp.int32, (SEQ, 128), 1)

    def split3(v):
        hi = v.astype(BF16).astype(F32)
        mid = (v - hi).astype(BF16).astype(F32)
        low = v - hi - mid
        return jnp.where(lane == 0, hi, jnp.where(lane == 1, mid, low)).astype(BF16)

    kv0 = kvm[0].astype(F32)
    kv1 = kvm[1].astype(F32)
    kvsnd[:, 0:KW] = jnp.where(swap, kv0, kv1).astype(BF16)
    kvsnd[:, KW:KX] = split3(invs[1])
    remote(kvsnd, kvall.at[1, slot], km_s.at[0], km_r.at[0], dev(7 - p, x, mir(c), c)).start()
    kvall[0, slot, :, 0:KW] = jnp.where(swap, kv1, kv0).astype(BF16)
    kvall[0, slot, :, KW:KX] = split3(invs[0])

    def spread_kv(e):
        mine = kvall.at[e, slot]
        for j in (1, 2, 3):
            xx = lax.rem(x + j, 4)
            remote(mine, mine, kx_s.at[e, j], kx_r.at[e, x], dev(p, xx, zh, c)).start()
        remote(mine, mine, kc_s.at[e, x], kc_r.at[e, x], dev(p, x, zh, 1 - c)).start()

    spread_kv(0)
    here(km_s.at[0], km_r.at[0], kvall.at[1, slot]).wait_recv()
    spread_kv(1)
    for e in range(2):
        for j in (1, 3, 2):
            xx = lax.rem(x + j, 4)
            got = kvall.at[e, xx * 2 + c]
            here(kx_s.at[e, j], kx_r.at[e, xx], got).wait_recv()
            remote(got, got, kc_s.at[e, xx], kc_r.at[e, xx], dev(p, x, zh, 1 - c)).start()

    here(w_s.at[0], w_r.at[0], wall.at[zm]).wait_recv()
    first = wall.at[zm, pl.ds(0, HALF)]
    remote(first, first, w_s.at[2], w_r.at[2], dev(p, x, zp, c)).start()
    here(w_s.at[1], w_r.at[1], wall.at[zp]).wait_recv()
    second = wall.at[zp, pl.ds(HALF, HALF)]
    remote(second, second, w_s.at[3], w_r.at[3], dev(p, x, zm, c)).start()

    own_norm.wait()

    def wait_norm(j):
        t = lax.rem(slot + j, 8)
        here(ns_s.at[1, t], ns_r.at[1, t], nrecv.at[1, t]).wait_recv()

        @pl.when(j > 0)
        def _():
            here(ns_s.at[0, t], ns_r.at[0, t], nrecv.at[0, t]).wait_recv()

    loop(0, 8, wait_norm)
    for e in range(2):
        for xx in range(4):
            here(kc_s.at[e, xx], kc_r.at[e, xx], kvall.at[e, xx * 2 + 1 - c]).wait_recv()
    for j, zz in ((1, zm), (2, zf), (3, zp)):
        here(g_s.at[j], g_r.at[j], gall.at[zz]).wait_recv()

    def weight_grad(b, store):
        g = gall[b, 0:1, :].astype(F32)
        for e in range(2):
            n = nrecv[e, :, b].reshape(8 * SEQ, BLK)
            hbuf[e * 8 * SEQ : (e + 1) * 8 * SEQ, :] = (n.astype(F32) * g).astype(BF16)

        def cols(i):
            cc = pl.ds(pl.multiple_of(i * BLK, BLK), BLK)
            kvc = kvall[:, :, :, cc].reshape(16 * SEQ, BLK)
            store(cc, dot(hbuf[...], kvc, 0, 0))

        loop(0, KW // BLK, cols)

    def to_far(cc, v):
        rsf_s[:, cc] = v.astype(BF16)

    weight_grad(zf, to_far)
    remote(rsf_s.at[pl.ds(0, HALF)], rsf_r.at[0], rs_s.at[0], rs_r.at[0], dev(p, x, zp, c)).start()
    remote(rsf_s.at[pl.ds(HALF, HALF)], rsf_r.at[1], rs_s.at[1], rs_r.at[1], dev(p, x, zm, c)).start()
    for i, b in enumerate((zp, zm, zh)):

        def to_part(cc, v, i=i):
            part[i, :, cc] = v

        weight_grad(b, to_part)

    here(w_s.at[2], w_r.at[2], wall.at[zf, pl.ds(0, HALF)]).wait_recv()
    here(w_s.at[3], w_r.at[3], wall.at[zf, pl.ds(HALF, HALF)]).wait_recv()
    cacc[...] = jnp.zeros_like(cacc)

    def hidden_grad(b):
        g = gall[b, 0:1, :].astype(F32)
        total = jnp.zeros((8, BLK), F32)
        for e in range(2):
            hg = dot(kvall[e, :, :, 0:KW].reshape(8 * SEQ, KW), wall[b], 1, 1)
            n = nrecv[e, :, b].reshape(8 * SEQ, BLK).astype(F32)
            total = total + jnp.sum((hg * n).reshape(SEQ, 8, BLK), axis=0)
            ng = (hg * g).astype(BF16)
            ngb[e, :, b] = ng.reshape(8, SEQ, BLK)
            t = ng.astype(F32) * n
            cacc[e] = cacc[e] + t[:, 0:128] + t[:, 128:256]
        gpart[b] = total

    loop(0, 4, hidden_grad)
    eye = lax.broadcasted_iota(jnp.int32, (128, 128), 0) == lax.broadcasted_iota(
        jnp.int32, (128, 128), 1
    )
    for e in range(2):
        for i in range(4):
            col = jnp.sum(cacc[e, i * 128 : (i + 1) * 128, :], axis=1, keepdims=True)
            c_s[e * 4 + i : e * 4 + i + 1, :] = jnp.sum(
                jnp.where(eye, col, 0.0), axis=0, keepdims=True
            )
    c_r[slot] = c_s[...]

    def send_c(j):
        t = lax.rem(slot + j, 8)
        remote(
            c_s, c_r.at[slot], c_ss.at[t], c_rs.at[slot], dev(p, lax.div(t, 2), zh, lax.rem(t, 2))
        ).start()

    loop(1, 8, send_c)
    for j, zz in ((1, zp), (2, zf), (3, zm)):
        remote(gpart.at[zz], gg_r.at[j], gg_ss.at[j], gg_rs.at[j], dev(p, x, zz, c)).start()

    here(rs_s.at[0], rs_r.at[0], rsf_r.at[0]).wait_recv()
    rsn_s[0, 0:HALF, :] = (part[0, 0:HALF, :] + rsf_r[0].astype(F32)).astype(BF16)
    rsn_s[0, HALF:BLK, :] = part[0, HALF:BLK, :].astype(BF16)
    remote(rsn_s.at[0], rsn_r.at[0], rs_s.at[2], rs_r.at[2], dev(p, x, zp, c)).start()
    here(rs_s.at[1], rs_r.at[1], rsf_r.at[1]).wait_recv()
    rsn_s[1, 0:HALF, :] = part[1, 0:HALF, :].astype(BF16)
    rsn_s[1, HALF:BLK, :] = (part[1, HALF:BLK, :] + rsf_r[1].astype(F32)).astype(BF16)
    remote(rsn_s.at[1], rsn_r.at[1], rs_s.at[3], rs_r.at[3], dev(p, x, zm, c)).start()

    def wait_c(j):
        t = lax.rem(slot + j, 8)
        here(c_ss.at[t], c_rs.at[t], c_r.at[t]).wait_recv()

    loop(1, 8, wait_c)
    mean = jnp.sum(c_r[...], axis=0) * (1.0 / D)
    for e in range(2):
        for i in range(4):
            row = mean[e * 4 + i : e * 4 + i + 1, :]
            col = jnp.sum(jnp.where(eye, row, 0.0), axis=1, keepdims=True)
            cbuf[e, 2 * i : 2 * i + 2] = jnp.broadcast_to(col, (128, 128)).reshape(2, SEQ, 128)

    @pl.when(jnp.logical_not(back_down))
    def _():
        brecv[0] = jnp.zeros_like(brecv[0])

    @pl.when(jnp.logical_not(back_up))
    def _():
        brecv[1] = jnp.zeros_like(brecv[1])

    def finish(j):
        t = lax.rem(slot + j, 8)
        xx = lax.div(t, 2)
        cc = lax.rem(t, 2)
        for e in range(2):
            mc = cbuf[e, t][:, 0:1]
            parts3 = kvall[e, t, :, KW:KX].astype(F32)
            inv = jnp.sum(jnp.where(lane < 3, parts3, 0.0), axis=1, keepdims=True)
            for b in range(4):
                n = nrecv[e, t, b].astype(F32)
                bsend[e, t, b] = (inv * (ngb[e, t, b].astype(F32) - n * mc)).astype(BF16)
        is_self = jnp.logical_and(self_up, j == 0)

        @pl.when(back_up)
        def _():
            remote(
                bsend.at[0, t], brecv.at[0, slot], b_s.at[0, t], b_r.at[0, slot], dev(p - 1, xx, zh, cc)
            ).start()

        @pl.when(jnp.logical_and(back_up, jnp.logical_not(is_self)))
        def _():
            remote(
                bsend.at[1, t],
                brecv.at[1, slot],
                b_s.at[1, t],
                b_r.at[1, slot],
                dev(8 - p, xx, mir(cc), cc),
            ).start()

        @pl.when(is_self)
        def _():
            pltpu.make_async_copy(bsend.at[1, t], brecv.at[1, slot], b_r.at[1, slot]).start()

    loop(0, 8, finish)

    here(rs_s.at[2], rs_r.at[2], rsn_r.at[0]).wait_recv()
    here(rs_s.at[3], rs_r.at[3], rsn_r.at[1]).wait_recv()
    wg = part[2] + rsn_r[0].astype(F32) + rsn_r[1].astype(F32)
    wk_out[...] = wg[:, 0:KVW]
    wv_out[...] = wg[:, KVW:KW]
    gg = gpart[zh]
    for j in (1, 2, 3):
        here(gg_ss.at[j], gg_rs.at[j], gg_r.at[j]).wait_recv()
        gg = gg + gg_r[j]
    gg_out[...] = jnp.sum(gg, axis=0, keepdims=True)

    def wait_back(t):
        @pl.when(back_down)
        def _():
            here(b_s.at[0, t], b_r.at[0, t], brecv.at[0, t]).wait_recv()

        @pl.when(back_up)
        def _():
            here(b_s.at[1, t], b_r.at[1, t], brecv.at[1, t]).wait_recv()

    loop(0, 8, wait_back)
    for j in range(32):
        t = (j // 8) * 2 + j % 2
        b = (j // 2) % 4
        down = brecv[0, t, b].astype(F32)
        up = brecv[1, t, b].astype(F32)
        passed_out[0, :, j * BLK : (j + 1) * BLK] = jnp.where(swap, up, down).astype(BF16)
        passed_out[1, :, j * BLK : (j + 1) * BLK] = jnp.where(swap, down, up).astype(BF16)

    def drain(t):
        here(ns_s.at[1, t], ns_r.at[1, t], nsend.at[1, t]).wait_send()

        @pl.when(t != slot)
        def _():
            here(ns_s.at[0, t], ns_r.at[0, t], nsend.at[0, t]).wait_send()
            here(c_ss.at[t], c_rs.at[t], c_s).wait_send()

        @pl.when(back_up)
        def _():
            here(b_s.at[0, t], b_r.at[0, t], bsend.at[0, t]).wait_send()

        @pl.when(jnp.logical_and(back_up, jnp.logical_not(jnp.logical_and(self_up, t == slot))))
        def _():
            here(b_s.at[1, t], b_r.at[1, t], bsend.at[1, t]).wait_send()

    loop(0, 8, drain)
    here(km_s.at[0], km_r.at[0], kvsnd).wait_send()
    for e in range(2):
        for j in (1, 2, 3):
            here(kx_s.at[e, j], kx_r.at[e, j], kvall.at[e, slot]).wait_send()
        for xx in range(4):
            here(kc_s.at[e, xx], kc_r.at[e, xx], kvall.at[e, xx * 2 + c]).wait_send()
    for j in (1, 2, 3):
        here(g_s.at[j], g_r.at[j], gall.at[zh]).wait_send()
        here(gg_ss.at[j], gg_rs.at[j], gg_r.at[j]).wait_send()
    here(w_s.at[0], w_r.at[0], wall.at[zh]).wait_send()
    here(w_s.at[1], w_r.at[1], wall.at[zh]).wait_send()
    here(w_s.at[2], w_r.at[2], first).wait_send()
    here(w_s.at[3], w_r.at[3], second).wait_send()
    here(rs_s.at[0], rs_r.at[0], rsf_r.at[0]).wait_send()
    here(rs_s.at[1], rs_r.at[1], rsf_r.at[1]).wait_send()
    here(rs_s.at[2], rs_r.at[2], rsn_s.at[0]).wait_send()
    here(rs_s.at[3], rs_r.at[3], rsn_s.at[1]).wait_send()


def on_device(
    queries,
    keys,
    values,
    out_grad,
    block_input,
    positions,
    direction,
    key_weight,
    value_weight,
    gain,
):
    vmem = pl.BlockSpec(memory_space=pltpu.VMEM)
    smem = pl.BlockSpec(memory_space=pltpu.SMEM)
    hbm = pl.BlockSpec(memory_space=pl.ANY)
    dma = pltpu.SemaphoreType.DMA
    scratch = [
        pltpu.VMEM((2, SEQ, QW), BF16),
        pltpu.VMEM((2, SEQ, QW), BF16),
        pltpu.VMEM((2, SEQ, D), BF16),
        pltpu.VMEM((2, 8, 4, SEQ, BLK), BF16),
        pltpu.VMEM((2, 8, 4, SEQ, BLK), BF16),
        pltpu.VMEM((2, SEQ, 128), F32),
        pltpu.VMEM((2, SEQ, SEQ), F32),
        pltpu.VMEM((2, SEQ, KW), BF16),
        pltpu.VMEM((SEQ, KX), BF16),
        pltpu.VMEM((2, 8, SEQ, KX), BF16),
        pltpu.VMEM((4, BLK, KW), BF16),
        pltpu.VMEM((4, 16, BLK), BF16),
        pltpu.VMEM((16 * SEQ, BLK), BF16),
        pltpu.VMEM((3, BLK, KW), F32),
        pltpu.VMEM((BLK, KW), BF16),
        pltpu.VMEM((2, HALF, KW), BF16),
        pltpu.VMEM((2, BLK, KW), BF16),
        pltpu.VMEM((2, BLK, KW), BF16),
        pltpu.VMEM((2, 8, 4, SEQ, BLK), BF16),
        pltpu.VMEM((2, 8 * SEQ, 128), F32),
        pltpu.VMEM((4, 8, BLK), F32),
        pltpu.VMEM((4, 8, BLK), F32),
        pltpu.VMEM((8, 128), F32),
        pltpu.VMEM((8, 8, 128), F32),
        pltpu.VMEM((2, 8, SEQ, 128), F32),
        pltpu.VMEM((2, 8, 4, SEQ, BLK), BF16),
        pltpu.VMEM((2, 8, 4, SEQ, BLK), BF16),
        dma((6,)),
        dma((2, 8)),
        dma((2, 8)),
        dma((4,)),
        dma((4,)),
        dma((1,)),
        dma((1,)),
        dma((2, 4)),
        dma((2, 4)),
        dma((2, 4)),
        dma((2, 4)),
        dma((4,)),
        dma((4,)),
        dma((4,)),
        dma((4,)),
        dma((4,)),
        dma((4,)),
        dma((8,)),
        dma((8,)),
        dma((2, 8)),
        dma((2, 8)),
    ]
    qg, passed, wk, wv, gg = pl.pallas_call(
        kernel,
        name="relay",
        out_shape=(
            jax.ShapeDtypeStruct((2, SEQ, QW), BF16),
            jax.ShapeDtypeStruct((2, SEQ, D), BF16),
            jax.ShapeDtypeStruct((BLK, KVW), F32),
            jax.ShapeDtypeStruct((BLK, KVW), F32),
            jax.ShapeDtypeStruct((1, BLK), F32),
        ),
        in_specs=[smem, vmem, vmem, vmem, vmem, hbm, hbm, hbm, hbm, hbm],
        out_specs=(vmem, vmem, vmem, vmem, vmem),
        scratch_shapes=scratch,
        compiler_params=pltpu.CompilerParams(
            collective_id=0, has_side_effects=True, vmem_limit_bytes=56 * 2**20
        ),
    )(
        direction,
        positions.reshape(2, 1, SEQ),
        keys[:, 0],
        values[:, 0],
        gain,
        queries[:, 0],
        out_grad[:, 0],
        block_input[:, 0],
        key_weight[0],
        value_weight[0],
    )
    return qg[:, None], passed[:, None], wk[None], wv[None], gg


def solution(mesh):
    in_specs = (
        P(None, "pipe", "dp", None),
        P(None, "pipe", "dp", None),
        P(None, "pipe", "dp", None),
        P(None, "pipe", "dp", None),
        P(None, "pipe", "dp", None),
        P(None, "pipe", "dp"),
        P(),
        P("pipe", "dp", None),
        P("pipe", "dp", None),
        P("pipe", "dp"),
    )
    out_specs = (
        P(None, "pipe", "dp", None),
        P(None, "pipe", "dp", None),
        P("pipe", "dp", None),
        P("pipe", "dp", None),
        P("pipe", "dp"),
    )
    return jax.shard_map(
        on_device, mesh=mesh, in_specs=in_specs, out_specs=out_specs, check_vma=False
    )
```

```python
import functools

import jax
import jax.numpy as jnp
from jax import lax
from jax.experimental import pallas as pl
from jax.experimental.pallas import tpu as pltpu
from jax.sharding import PartitionSpec as P

KVH = 4
HD = 128
GROUP = 8
SEQ = 64
QW = 4096
KVW = 512
D = 8192
BLK = 256
KW = 2 * KVW
KX = KW + 128
HALF = BLK // 2
MOST = HALF + HALF // 2
MESH = pl.DeviceIdType.MESH
F32 = jnp.float32
BF16 = jnp.bfloat16


def dot(a, b, ca, cb):
    return lax.dot_general(a, b, (((ca,), (cb,)), ((), ())), preferred_element_type=F32)


def kernel(
    flag,
    pos,
    keys,
    values,
    gain,
    q_hbm,
    og_hbm,
    inp_hbm,
    kw_hbm,
    vw_hbm,
    qg_hbm,
    passed_out,
    wk_out,
    wv_out,
    gg_out,
    qg,
    q,
    og,
    inp,
    nsend,
    nrecv,
    invs,
    vis,
    kvm,
    kvsnd,
    kvall,
    wall,
    gall,
    hbuf,
    part,
    own,
    rsf_s,
    rsf_r,
    rsn_s,
    rsn_r,
    ngb,
    cacc,
    gpart,
    gg_r,
    c_s,
    c_r,
    cbuf,
    bsend,
    brecv,
    relay,
    lsem,
    ns_s,
    ns_r,
    g_s,
    g_r,
    km_s,
    km_r,
    kx_s,
    kx_r,
    kc_s,
    kc_r,
    w_s,
    w_r,
    rs_s,
    rs_r,
    gg_ss,
    gg_rs,
    c_ss,
    c_rs,
    b_s,
    b_r,
    u_s,
    u_r,
):
    p = lax.axis_index("pipe")
    d = lax.axis_index("dp")
    zl = lax.div(p, 4)
    x = lax.div(d, 8)
    zh = lax.rem(lax.div(d, 2), 4)
    c = lax.rem(d, 2)
    slot = x * 2 + c
    zp = lax.rem(zh + 1, 4)
    zf = lax.rem(zh + 2, 4)
    zm = lax.rem(zh + 3, 4)

    def dev(pp, xx, zz, cc):
        return (pp, xx * 8 + zz * 2 + cc)

    def mir(cc):
        return lax.rem(zh + 4 + cc * (2 * zl - 1), 4)

    def remote(src, dst, ss, rs, to):
        return pltpu.make_async_remote_copy(
            src_ref=src, dst_ref=dst, send_sem=ss, recv_sem=rs, device_id=to, device_id_type=MESH
        )

    def here(ss, rs, ref):
        return remote(ref, ref, ss, rs, dev(p, x, zh, 1 - c))

    def loop(lo, hi, f):
        def step(i, carry):
            f(i)
            return carry

        lax.fori_loop(lo, hi, step, 0)

    load_inp = pltpu.make_async_copy(inp_hbm, inp, lsem.at[0])
    load_kw = pltpu.make_async_copy(kw_hbm, wall.at[zh, :, pl.ds(0, KVW)], lsem.at[1])
    load_vw = pltpu.make_async_copy(vw_hbm, wall.at[zh, :, pl.ds(KVW, KVW)], lsem.at[2])
    load_q = pltpu.make_async_copy(q_hbm, q, lsem.at[3])
    load_og = pltpu.make_async_copy(og_hbm, og, lsem.at[4])
    load_kw.start()
    load_vw.start()
    load_inp.start()
    load_q.start()
    load_og.start()

    bar = pltpu.get_barrier_semaphore()

    def greet(to):
        pl.semaphore_signal(bar, inc=1, device_id=to, device_id_type=MESH)

    back_up = p >= 1
    back_down = p <= 6
    self_up = jnp.logical_and(p == 4, c == 0)
    zlm = lax.div(p + 3, 4) - 1
    zup = lax.rem(zh + 4 + c * (2 * zlm - 1), 4)

    even = lax.rem(p, 2) == 0
    odd = jnp.logical_not(even)
    even_up = jnp.logical_and(even, back_up)
    for zz in (zp, zm, zf):
        greet(dev(p, x, zz, c))

    @pl.when(odd)
    def _():
        greet(dev(p - 1, x, zh, c))

    def greet_all(j):
        t = lax.rem(slot + j, 8)
        xx = lax.div(t, 2)
        cc = lax.rem(t, 2)

        @pl.when(j > 0)
        def _():
            greet(dev(p, xx, zh, cc))

        greet(dev(7 - p, xx, mir(cc), cc))

        @pl.when(back_down)
        def _():
            greet(dev(p + 1, xx, zh, cc))

        @pl.when(even)
        def _():
            greet(dev(7 - p, xx, mir(c), cc))

        @pl.when(jnp.logical_and(even_up, jnp.logical_not(jnp.logical_and(self_up, j == 0))))
        def _():
            greet(dev(8 - p, xx, zup, cc))

    loop(0, 8, greet_all)
    gall[zh] = jnp.broadcast_to(gain[...], (16, BLK))

    swap = flag[0] == 1
    load_inp.wait()

    def norm_rows(i):
        r = pl.ds(pl.multiple_of(i * 16, 16), 16)
        sq = [jnp.zeros((16, BLK), F32), jnp.zeros((16, BLK), F32)]
        for j in range(32):
            for m in range(2):
                v = inp[m, r, j * BLK : (j + 1) * BLK].astype(F32)
                sq[m] = sq[m] + v * v
        inv = [lax.rsqrt(jnp.sum(s, axis=1, keepdims=True) * (1.0 / D) + 1e-05) for s in sq]
        for j in range(32):
            t = (j // 8) * 2 + j % 2
            b = (j // 2) % 4
            v0 = inp[0, r, j * BLK : (j + 1) * BLK].astype(F32) * inv[0]
            v1 = inp[1, r, j * BLK : (j + 1) * BLK].astype(F32) * inv[1]
            nsend[0, t, b, r, :] = jnp.where(swap, v1, v0).astype(BF16)
            nsend[1, t, b, r, :] = jnp.where(swap, v0, v1).astype(BF16)
        i0 = jnp.broadcast_to(inv[0], (16, 128))
        i1 = jnp.broadcast_to(inv[1], (16, 128))
        invs[0, r, :] = jnp.where(swap, i1, i0)
        invs[1, r, :] = jnp.where(swap, i0, i1)

    loop(0, SEQ // 16, norm_rows)

    n_back = jnp.where(back_up, 16, 0) - jnp.where(self_up, 1, 0) + jnp.where(even, 1, 0)
    pl.semaphore_wait(bar, 18 + n_back)

    low = pl.ds(0, HALF)
    high = pl.ds(HALF, HALF)

    def send_w(zz, part_rows, i, to):
        ref = wall.at[zz, part_rows]
        remote(ref, ref, w_s.at[i], w_r.at[i], dev(p, x, to, c)).start()

    load_kw.wait()
    load_vw.wait()
    send_w(zh, low, 0, zp)
    send_w(zh, high, 3, zm)
    send_w(zh, high, 1, zp)
    send_w(zh, low, 2, zm)
    for j, zz in ((1, zp), (2, zf), (3, zm)):
        remote(gall.at[zh], gall.at[zh], g_s.at[j], g_r.at[j], dev(p, x, zz, c)).start()

    eye64 = lax.broadcasted_iota(jnp.int32, (SEQ, SEQ), 0) == lax.broadcasted_iota(
        jnp.int32, (SEQ, SEQ), 1
    )
    row_id = lax.broadcasted_iota(jnp.int32, (SEQ, SEQ), 0)
    col_id = lax.broadcasted_iota(jnp.int32, (SEQ, SEQ), 1)
    for m in range(2):
        start_row = (col_id - pos[m]).astype(F32)
        start_col = jnp.sum(jnp.where(eye64, start_row, 0.0), axis=1, keepdims=True)
        seen = jnp.logical_and(row_id >= col_id, start_row == start_col)
        vis[m] = jnp.where(seen, 1.0, 0.0)
    load_q.wait()
    load_og.wait()
    scale = HD ** (-0.5)

    def attend(i):
        m = lax.div(i, KVH)
        k = lax.rem(i, KVH)
        cols = pl.ds(pl.multiple_of(k * HD, HD), HD)
        heads = [
            pl.ds(pl.multiple_of(k * (GROUP * HD) + g * HD, HD), HD) for g in range(GROUP)
        ]
        kk = keys[m, :, cols]
        vv = values[m, :, cols]
        qs = jnp.concatenate([q[m, :, h] for h in heads], axis=0)
        gs = jnp.concatenate([og[m, :, h] for h in heads], axis=0)
        seen = jnp.concatenate([vis[m]] * GROUP, axis=0) > 0.5
        s = jnp.where(seen, dot(qs, kk, 1, 1) * scale, -1e30)
        w = jnp.exp(s - jnp.max(s, axis=1, keepdims=True))
        probs = w / jnp.sum(w, axis=1, keepdims=True)
        pb = probs.astype(BF16)
        attn = dot(pb, vv, 1, 0).astype(BF16)
        delta = jnp.sum(gs.astype(F32) * attn.astype(F32), axis=1, keepdims=True)
        ds = (probs * (dot(gs, vv, 1, 1) - delta)).astype(BF16)
        qgs = (dot(ds, kk, 1, 0) * scale).astype(BF16)
        for g, h in enumerate(heads):
            qg[m, :, h] = qgs[g * SEQ : (g + 1) * SEQ]
        kvm[m, :, cols] = (dot(ds, qs, 0, 0) * scale).astype(BF16)
        kvm[m, :, pl.ds(pl.multiple_of(KVW + k * HD, HD), HD)] = dot(pb, gs, 0, 0).astype(BF16)

    loop(0, 2 * KVH, attend)
    store_qg = pltpu.make_async_copy(qg, qg_hbm, lsem.at[6])
    store_qg.start()

    lane = lax.broadcasted_iota(jnp.int32, (SEQ, 128), 1)

    def split3(v):
        hi = v.astype(BF16).astype(F32)
        mid = (v - hi).astype(BF16).astype(F32)
        low = v - hi - mid
        return jnp.where(lane == 0, hi, jnp.where(lane == 1, mid, low)).astype(BF16)

    kv0 = kvm[0].astype(F32)
    kv1 = kvm[1].astype(F32)
    kvsnd[:, 0:KW] = jnp.where(swap, kv0, kv1).astype(BF16)
    kvsnd[:, KW:KX] = split3(invs[1])
    remote(kvsnd, kvall.at[1, slot], km_s.at[0], km_r.at[0], dev(7 - p, x, mir(c), c)).start()
    kvall[0, slot, :, 0:KW] = jnp.where(swap, kv1, kv0).astype(BF16)
    kvall[0, slot, :, KW:KX] = split3(invs[0])

    def spread_kv(e):
        mine = kvall.at[e, slot]
        for j in (1, 2, 3):
            xx = lax.rem(x + j, 4)
            remote(mine, mine, kx_s.at[e, j], kx_r.at[e, x], dev(p, xx, zh, c)).start()
        remote(mine, mine, kc_s.at[e, x], kc_r.at[e, x], dev(p, x, zh, 1 - c)).start()

    spread_kv(0)

    def send_norm(j):
        t = lax.rem(slot + j, 8)
        xx = lax.div(t, 2)
        cc = lax.rem(t, 2)
        remote(
            nsend.at[1, t], nrecv.at[1, slot], ns_s.at[1, t], ns_r.at[1, slot], dev(7 - p, xx, mir(c), cc)
        ).start()

        @pl.when(j > 0)
        def _():
            remote(
                nsend.at[0, t], nrecv.at[0, slot], ns_s.at[0, t], ns_r.at[0, slot], dev(p, xx, zh, cc)
            ).start()

    loop(0, 8, send_norm)
    own_norm = pltpu.make_async_copy(nsend.at[0, slot], nrecv.at[0, slot], lsem.at[5])
    own_norm.start()

    here(km_s.at[0], km_r.at[0], kvall.at[1, slot]).wait_recv()
    spread_kv(1)
    def got_w(zz, part_rows, i):
        here(w_s.at[i], w_r.at[i], wall.at[zz, part_rows]).wait_recv()

    got_w(zm, low, 0)
    send_w(zm, low, 4, zp)
    got_w(zp, high, 3)
    send_w(zp, high, 5, zm)

    for e in range(2):
        for j in (1, 3, 2):
            xx = lax.rem(x + j, 4)
            got = kvall.at[e, xx * 2 + c]
            here(kx_s.at[e, j], kx_r.at[e, xx], got).wait_recv()
            remote(got, got, kc_s.at[e, xx], kc_r.at[e, xx], dev(p, x, zh, 1 - c)).start()

    own_norm.wait()

    def wait_norm(j):
        t = lax.rem(slot + j, 8)
        here(ns_s.at[1, t], ns_r.at[1, t], nrecv.at[1, t]).wait_recv()

        @pl.when(j > 0)
        def _():
            here(ns_s.at[0, t], ns_r.at[0, t], nrecv.at[0, t]).wait_recv()

    loop(0, 8, wait_norm)
    for e in range(2):
        for xx in range(4):
            here(kc_s.at[e, xx], kc_r.at[e, xx], kvall.at[e, xx * 2 + 1 - c]).wait_recv()
    for j, zz in ((1, zm), (2, zf), (3, zp)):
        here(g_s.at[j], g_r.at[j], gall.at[zz]).wait_recv()

    def weight_grad(b, store):
        g = gall[b, 0:1, :].astype(F32)
        for e in range(2):
            n = nrecv[e, :, b].reshape(8 * SEQ, BLK)
            hbuf[e * 8 * SEQ : (e + 1) * 8 * SEQ, :] = (n.astype(F32) * g).astype(BF16)

        def cols(i):
            cc = pl.ds(pl.multiple_of(i * BLK, BLK), BLK)
            kvc = kvall[:, :, :, cc].reshape(16 * SEQ, BLK)
            store(cc, dot(hbuf[...], kvc, 0, 0))

        loop(0, KW // BLK, cols)

    def send_rs(src, dst, i, to):
        remote(src, dst, rs_s.at[i], rs_r.at[i], dev(p, x, to, c)).start()

    def to_far(cc, v):
        rsf_s[:, cc] = v.astype(BF16)

    def to_next(cc, v):
        part[0, 0:MOST, cc] = v[0:MOST]
        rsn_s[0, MOST:BLK, cc] = v[MOST:BLK].astype(BF16)

    def to_prev(cc, v):
        part[1, 0:HALF, cc] = v[HALF:BLK]
        rsn_s[1, 0:HALF, cc] = v[0:HALF].astype(BF16)

    def to_own(cc, v):
        own[:, cc] = v

    third = pl.ds(HALF, HALF // 2)
    fourth = pl.ds(HALF + HALF // 2, HALF // 2)
    upward = lax.rem(p, 4) == 0
    weight_grad(zf, to_far)
    send_rs(rsf_s.at[low], rsf_r.at[low], 0, zp)
    send_rs(rsf_s.at[third], rsf_r.at[third], 1, jnp.where(upward, zp, zm))
    send_rs(rsf_s.at[fourth], rsf_r.at[fourth], 2, zm)
    weight_grad(zp, to_next)
    send_rs(rsn_s.at[0, fourth], rsn_r.at[0, fourth], 3, zp)
    weight_grad(zm, to_prev)
    send_rs(rsn_s.at[1, low], rsn_r.at[1, low], 4, zm)

    got_w(zm, high, 1)
    got_w(zp, low, 2)
    got_w(zf, low, 4)
    got_w(zf, high, 5)
    cacc[...] = jnp.zeros_like(cacc)

    def hidden_grad(b):
        g = gall[b, 0:1, :].astype(F32)
        total = jnp.zeros((8, BLK), F32)
        for e in range(2):
            hg = dot(kvall[e, :, :, 0:KW].reshape(8 * SEQ, KW), wall[b], 1, 1)
            n = nrecv[e, :, b].reshape(8 * SEQ, BLK).astype(F32)
            total = total + jnp.sum((hg * n).reshape(SEQ, 8, BLK), axis=0)
            ng = (hg * g).astype(BF16)
            ngb[e, :, b] = ng.reshape(8, SEQ, BLK)
            t = ng.astype(F32) * n
            cacc[e] = cacc[e] + t[:, 0:128] + t[:, 128:256]
        gpart[b] = total

    loop(0, 4, hidden_grad)
    eye = lax.broadcasted_iota(jnp.int32, (128, 128), 0) == lax.broadcasted_iota(
        jnp.int32, (128, 128), 1
    )
    for e in range(2):
        for i in range(4):
            col = jnp.sum(cacc[e, i * 128 : (i + 1) * 128, :], axis=1, keepdims=True)
            c_s[e * 4 + i : e * 4 + i + 1, :] = jnp.sum(
                jnp.where(eye, col, 0.0), axis=0, keepdims=True
            )
    c_r[slot] = c_s[...]

    def send_c(j):
        t = lax.rem(slot + j, 8)
        remote(
            c_s, c_r.at[slot], c_ss.at[t], c_rs.at[slot], dev(p, lax.div(t, 2), zh, lax.rem(t, 2))
        ).start()

    loop(1, 8, send_c)
    for j, zz in ((1, zp), (2, zf), (3, zm)):
        remote(gpart.at[zz], gg_r.at[j], gg_ss.at[j], gg_rs.at[j], dev(p, x, zz, c)).start()

    def wait_c(j):
        t = lax.rem(slot + j, 8)
        here(c_ss.at[t], c_rs.at[t], c_r.at[t]).wait_recv()

    loop(1, 8, wait_c)
    mean = jnp.sum(c_r[...], axis=0) * (1.0 / D)
    for e in range(2):
        for i in range(4):
            row = mean[e * 4 + i : e * 4 + i + 1, :]
            col = jnp.sum(jnp.where(eye, row, 0.0), axis=1, keepdims=True)
            cbuf[e, 2 * i : 2 * i + 2] = jnp.broadcast_to(col, (128, 128)).reshape(2, SEQ, 128)

    @pl.when(jnp.logical_not(back_down))
    def _():
        brecv[0] = jnp.zeros_like(brecv[0])

    @pl.when(jnp.logical_not(back_up))
    def _():
        brecv[1] = jnp.zeros_like(brecv[1])

    def finish(j):
        t = lax.rem(slot + j, 8)
        xx = lax.div(t, 2)
        cc = lax.rem(t, 2)
        for e in range(2):
            mc = cbuf[e, t][:, 0:1]
            parts3 = kvall[e, t, :, KW:KX].astype(F32)
            inv = jnp.sum(jnp.where(lane < 3, parts3, 0.0), axis=1, keepdims=True)
            for b in range(4):
                n = nrecv[e, t, b].astype(F32)
                bsend[e, t, b] = (inv * (ngb[e, t, b].astype(F32) - n * mc)).astype(BF16)
        is_self = jnp.logical_and(self_up, j == 0)

        @pl.when(back_up)
        def _():
            remote(
                bsend.at[0, t], brecv.at[0, slot], b_s.at[0, t], b_r.at[0, slot], dev(p - 1, xx, zh, cc)
            ).start()

        @pl.when(odd)
        def _():
            remote(
                bsend.at[1, t], relay.at[slot], b_s.at[1, t], u_r.at[slot], dev(7 - p, xx, mir(cc), cc)
            ).start()

        @pl.when(jnp.logical_and(even_up, jnp.logical_not(is_self)))
        def _():
            remote(
                bsend.at[1, t],
                brecv.at[1, slot],
                b_s.at[1, t],
                b_r.at[1, slot],
                dev(8 - p, xx, mir(cc), cc),
            ).start()

        @pl.when(is_self)
        def _():
            pltpu.make_async_copy(bsend.at[1, t], brecv.at[1, slot], b_r.at[1, slot]).start()

    loop(0, 8, finish)

    here(rs_s.at[0], rs_r.at[0], rsf_r.at[low]).wait_recv()
    rsn_s[0, 0:HALF, :] = (part[0, 0:HALF, :] + rsf_r[0:HALF, :].astype(F32)).astype(BF16)
    send_rs(rsn_s.at[0, low], rsn_r.at[0, low], 5, zp)
    here(rs_s.at[1], rs_r.at[1], rsf_r.at[third]).wait_recv()
    more = rsf_r[HALF:MOST, :].astype(F32)
    rsn_s[0, HALF:MOST, :] = (part[0, HALF:MOST, :] + jnp.where(upward, more, 0.0)).astype(BF16)
    send_rs(rsn_s.at[0, third], rsn_r.at[0, third], 7, zp)
    rsn_s[1, HALF:MOST, :] = (part[1, 0 : MOST - HALF, :] + jnp.where(upward, 0.0, more)).astype(BF16)
    send_rs(rsn_s.at[1, third], rsn_r.at[1, third], 8, zm)
    here(rs_s.at[2], rs_r.at[2], rsf_r.at[fourth]).wait_recv()
    rsn_s[1, MOST:BLK, :] = (part[1, MOST - HALF : HALF, :] + rsf_r[MOST:BLK, :].astype(F32)).astype(BF16)
    send_rs(rsn_s.at[1, fourth], rsn_r.at[1, fourth], 6, zm)

    weight_grad(zh, to_own)

    def pass_on(t):
        here(u_s.at[t], u_r.at[t], relay.at[t]).wait_recv()
        remote(relay.at[t], brecv.at[1, t], u_s.at[t], b_r.at[1, t], dev(p + 1, x, zh, c)).start()

    @pl.when(even)
    def _():
        loop(0, 8, pass_on)

    near = ((3, 0, fourth), (4, 1, low), (5, 0, low), (6, 1, fourth), (7, 0, third), (8, 1, third))
    for i, side, piece in near:
        here(rs_s.at[i], rs_r.at[i], rsn_r.at[side, piece]).wait_recv()
    wg = own[...] + rsn_r[0].astype(F32) + rsn_r[1].astype(F32)
    wk_out[...] = wg[:, 0:KVW]
    wv_out[...] = wg[:, KVW:KW]
    gg = gpart[zh]
    for j in (1, 2, 3):
        here(gg_ss.at[j], gg_rs.at[j], gg_r.at[j]).wait_recv()
        gg = gg + gg_r[j]
    gg_out[...] = jnp.sum(gg, axis=0, keepdims=True)

    def wait_back(t):
        @pl.when(back_down)
        def _():
            here(b_s.at[0, t], b_r.at[0, t], brecv.at[0, t]).wait_recv()

        @pl.when(back_up)
        def _():
            here(b_s.at[1, t], b_r.at[1, t], brecv.at[1, t]).wait_recv()

    loop(0, 8, wait_back)
    for j in range(32):
        t = (j // 8) * 2 + j % 2
        b = (j // 2) % 4
        down = brecv[0, t, b].astype(F32)
        up = brecv[1, t, b].astype(F32)
        passed_out[0, :, j * BLK : (j + 1) * BLK] = jnp.where(swap, up, down).astype(BF16)
        passed_out[1, :, j * BLK : (j + 1) * BLK] = jnp.where(swap, down, up).astype(BF16)

    def drain(t):
        here(ns_s.at[1, t], ns_r.at[1, t], nsend.at[1, t]).wait_send()

        @pl.when(t != slot)
        def _():
            here(ns_s.at[0, t], ns_r.at[0, t], nsend.at[0, t]).wait_send()
            here(c_ss.at[t], c_rs.at[t], c_s).wait_send()

        @pl.when(even)
        def _():
            here(u_s.at[t], u_r.at[t], relay.at[t]).wait_send()

        @pl.when(back_up)
        def _():
            here(b_s.at[0, t], b_r.at[0, t], bsend.at[0, t]).wait_send()

        @pl.when(jnp.logical_and(back_up, jnp.logical_not(jnp.logical_and(self_up, t == slot))))
        def _():
            here(b_s.at[1, t], b_r.at[1, t], bsend.at[1, t]).wait_send()

    loop(0, 8, drain)
    here(km_s.at[0], km_r.at[0], kvsnd).wait_send()
    for e in range(2):
        for j in (1, 2, 3):
            here(kx_s.at[e, j], kx_r.at[e, j], kvall.at[e, slot]).wait_send()
        for xx in range(4):
            here(kc_s.at[e, xx], kc_r.at[e, xx], kvall.at[e, xx * 2 + c]).wait_send()
    for j in (1, 2, 3):
        here(g_s.at[j], g_r.at[j], gall.at[zh]).wait_send()
        here(gg_ss.at[j], gg_rs.at[j], gg_r.at[j]).wait_send()
    for i in range(6):
        here(w_s.at[i], w_r.at[i], wall.at[zh, low]).wait_send()
    for i, piece in ((0, low), (1, third), (2, fourth)):
        here(rs_s.at[i], rs_r.at[i], rsf_s.at[piece]).wait_send()
    for i, side, piece in near:
        here(rs_s.at[i], rs_r.at[i], rsn_s.at[side, piece]).wait_send()
    store_qg.wait()


def on_device(
    queries,
    keys,
    values,
    out_grad,
    block_input,
    positions,
    direction,
    key_weight,
    value_weight,
    gain,
):
    vmem = pl.BlockSpec(memory_space=pltpu.VMEM)
    smem = pl.BlockSpec(memory_space=pltpu.SMEM)
    hbm = pl.BlockSpec(memory_space=pl.ANY)
    dma = pltpu.SemaphoreType.DMA
    scratch = [
        pltpu.VMEM((2, SEQ, QW), BF16),
        pltpu.VMEM((2, SEQ, QW), BF16),
        pltpu.VMEM((2, SEQ, QW), BF16),
        pltpu.VMEM((2, SEQ, D), BF16),
        pltpu.VMEM((2, 8, 4, SEQ, BLK), BF16),
        pltpu.VMEM((2, 8, 4, SEQ, BLK), BF16),
        pltpu.VMEM((2, SEQ, 128), F32),
        pltpu.VMEM((2, SEQ, SEQ), F32),
        pltpu.VMEM((2, SEQ, KW), BF16),
        pltpu.VMEM((SEQ, KX), BF16),
        pltpu.VMEM((2, 8, SEQ, KX), BF16),
        pltpu.VMEM((4, BLK, KW), BF16),
        pltpu.VMEM((4, 16, BLK), BF16),
        pltpu.VMEM((16 * SEQ, BLK), BF16),
        pltpu.VMEM((2, MOST, KW), F32),
        pltpu.VMEM((BLK, KW), F32),
        pltpu.VMEM((BLK, KW), BF16),
        pltpu.VMEM((BLK, KW), BF16),
        pltpu.VMEM((2, BLK, KW), BF16),
        pltpu.VMEM((2, BLK, KW), BF16),
        pltpu.VMEM((2, 8, 4, SEQ, BLK), BF16),
        pltpu.VMEM((2, 8 * SEQ, 128), F32),
        pltpu.VMEM((4, 8, BLK), F32),
        pltpu.VMEM((4, 8, BLK), F32),
        pltpu.VMEM((8, 128), F32),
        pltpu.VMEM((8, 8, 128), F32),
        pltpu.VMEM((2, 8, SEQ, 128), F32),
        pltpu.VMEM((2, 8, 4, SEQ, BLK), BF16),
        pltpu.VMEM((2, 8, 4, SEQ, BLK), BF16),
        pltpu.VMEM((8, 4, SEQ, BLK), BF16),
        dma((7,)),
        dma((2, 8)),
        dma((2, 8)),
        dma((4,)),
        dma((4,)),
        dma((1,)),
        dma((1,)),
        dma((2, 4)),
        dma((2, 4)),
        dma((2, 4)),
        dma((2, 4)),
        dma((6,)),
        dma((6,)),
        dma((9,)),
        dma((9,)),
        dma((4,)),
        dma((4,)),
        dma((8,)),
        dma((8,)),
        dma((2, 8)),
        dma((2, 8)),
        dma((8,)),
        dma((8,)),
    ]
    qg, passed, wk, wv, gg = pl.pallas_call(
        kernel,
        name="relay",
        out_shape=(
            jax.ShapeDtypeStruct((2, SEQ, QW), BF16),
            jax.ShapeDtypeStruct((2, SEQ, D), BF16),
            jax.ShapeDtypeStruct((BLK, KVW), F32),
            jax.ShapeDtypeStruct((BLK, KVW), F32),
            jax.ShapeDtypeStruct((1, BLK), F32),
        ),
        in_specs=[smem, vmem, vmem, vmem, vmem, hbm, hbm, hbm, hbm, hbm],
        out_specs=(hbm, vmem, vmem, vmem, vmem),
        scratch_shapes=scratch,
        compiler_params=pltpu.CompilerParams(
            collective_id=0, has_side_effects=True, vmem_limit_bytes=56 * 2**20
        ),
    )(
        direction,
        positions.reshape(2, 1, SEQ),
        keys[:, 0],
        values[:, 0],
        gain,
        queries[:, 0],
        out_grad[:, 0],
        block_input[:, 0],
        key_weight[0],
        value_weight[0],
    )
    return qg[:, None], passed[:, None], wk[None], wv[None], gg


def solution(mesh):
    in_specs = (
        P(None, "pipe", "dp", None),
        P(None, "pipe", "dp", None),
        P(None, "pipe", "dp", None),
        P(None, "pipe", "dp", None),
        P(None, "pipe", "dp", None),
        P(None, "pipe", "dp"),
        P(),
        P("pipe", "dp", None),
        P("pipe", "dp", None),
        P("pipe", "dp"),
    )
    out_specs = (
        P(None, "pipe", "dp", None),
        P(None, "pipe", "dp", None),
        P("pipe", "dp", None),
        P("pipe", "dp", None),
        P("pipe", "dp"),
    )
    return jax.shard_map(
        on_device, mesh=mesh, in_specs=in_specs, out_specs=out_specs, check_vma=False
    )
```

```python
import functools

import jax
import jax.numpy as jnp
from jax import lax
from jax.experimental import pallas as pl
from jax.experimental.pallas import tpu as pltpu
from jax.sharding import PartitionSpec as P

KVH = 4
HD = 128
GROUP = 8
SEQ = 64
QW = 4096
KVW = 512
D = 8192
BLK = 256
KW = 2 * KVW
KX = KW + 128
HALF = BLK // 2
MOST = HALF + HALF // 2
MESH = pl.DeviceIdType.MESH
F32 = jnp.float32
BF16 = jnp.bfloat16


def dot(a, b, ca, cb):
    return lax.dot_general(a, b, (((ca,), (cb,)), ((), ())), preferred_element_type=F32)


def kernel(
    flag,
    pos,
    keys,
    values,
    gain,
    q_hbm,
    og_hbm,
    inp_hbm,
    kw_hbm,
    vw_hbm,
    qg_hbm,
    passed_out,
    wk_out,
    wv_out,
    gg_out,
    qg,
    q,
    og,
    inp,
    nsend,
    nrecv,
    invs,
    vis,
    kvm,
    kvsnd,
    kvall,
    wall,
    gall,
    hbuf,
    part,
    own,
    rsf_s,
    rsf_r,
    rsn_s,
    rsn_r,
    ngb,
    cacc,
    gpart,
    gsum,
    gg_r,
    c_s,
    c_r,
    cbuf,
    bsend,
    brecv,
    relay,
    lsem,
    ns_s,
    ns_r,
    g_s,
    g_r,
    km_s,
    km_r,
    kx_s,
    kx_r,
    kc_s,
    kc_r,
    w_s,
    w_r,
    rs_s,
    rs_r,
    gg_ss,
    gg_rs,
    c_ss,
    c_rs,
    b_s,
    b_r,
    u_s,
    u_r,
):
    p = lax.axis_index("pipe")
    d = lax.axis_index("dp")
    zl = lax.div(p, 4)
    x = lax.div(d, 8)
    zh = lax.rem(lax.div(d, 2), 4)
    c = lax.rem(d, 2)
    slot = x * 2 + c
    zp = lax.rem(zh + 1, 4)
    zf = lax.rem(zh + 2, 4)
    zm = lax.rem(zh + 3, 4)

    def dev(pp, xx, zz, cc):
        return (pp, xx * 8 + zz * 2 + cc)

    def mir(cc):
        return lax.rem(zh + 4 + cc * (2 * zl - 1), 4)

    def remote(src, dst, ss, rs, to):
        return pltpu.make_async_remote_copy(
            src_ref=src, dst_ref=dst, send_sem=ss, recv_sem=rs, device_id=to, device_id_type=MESH
        )

    def here(ss, rs, ref):
        return remote(ref, ref, ss, rs, dev(p, x, zh, 1 - c))

    def loop(lo, hi, f):
        def step(i, carry):
            f(i)
            return carry

        lax.fori_loop(lo, hi, step, 0)

    load_inp = pltpu.make_async_copy(inp_hbm, inp, lsem.at[0])
    load_kw = pltpu.make_async_copy(kw_hbm, wall.at[zh, :, pl.ds(0, KVW)], lsem.at[1])
    load_vw = pltpu.make_async_copy(vw_hbm, wall.at[zh, :, pl.ds(KVW, KVW)], lsem.at[2])
    load_q = pltpu.make_async_copy(q_hbm, q, lsem.at[3])
    load_og = pltpu.make_async_copy(og_hbm, og, lsem.at[4])
    load_kw.start()
    load_vw.start()
    load_inp.start()
    load_q.start()
    load_og.start()

    bar = pltpu.get_barrier_semaphore()

    def greet(to):
        pl.semaphore_signal(bar, inc=1, device_id=to, device_id_type=MESH)

    back_up = p >= 1
    back_down = p <= 6
    self_up = jnp.logical_and(p == 4, c == 0)
    zlm = lax.div(p + 3, 4) - 1
    zup = lax.rem(zh + 4 + c * (2 * zlm - 1), 4)

    even = lax.rem(p, 2) == 0
    odd = jnp.logical_not(even)
    even_up = jnp.logical_and(even, back_up)
    for zz in (zp, zm, zf):
        greet(dev(p, x, zz, c))

    @pl.when(odd)
    def _():
        greet(dev(p - 1, x, zh, c))

    def greet_all(j):
        t = lax.rem(slot + j, 8)
        xx = lax.div(t, 2)
        cc = lax.rem(t, 2)

        @pl.when(j > 0)
        def _():
            greet(dev(p, xx, zh, cc))

        greet(dev(7 - p, xx, mir(cc), cc))

        @pl.when(back_down)
        def _():
            greet(dev(p + 1, xx, zh, cc))

        @pl.when(even)
        def _():
            greet(dev(7 - p, xx, mir(c), cc))

        @pl.when(jnp.logical_and(even_up, jnp.logical_not(jnp.logical_and(self_up, j == 0))))
        def _():
            greet(dev(8 - p, xx, zup, cc))

    loop(0, 8, greet_all)
    gall[zh] = jnp.broadcast_to(gain[...], (16, BLK))

    swap = flag[0] == 1
    load_inp.wait()

    def norm_rows(i):
        r = pl.ds(pl.multiple_of(i * 16, 16), 16)
        sq = [jnp.zeros((16, BLK), F32), jnp.zeros((16, BLK), F32)]
        for j in range(32):
            for m in range(2):
                v = inp[m, r, j * BLK : (j + 1) * BLK].astype(F32)
                sq[m] = sq[m] + v * v
        inv = [lax.rsqrt(jnp.sum(s, axis=1, keepdims=True) * (1.0 / D) + 1e-05) for s in sq]
        for j in range(32):
            t = (j // 8) * 2 + j % 2
            b = (j // 2) % 4
            v0 = inp[0, r, j * BLK : (j + 1) * BLK].astype(F32) * inv[0]
            v1 = inp[1, r, j * BLK : (j + 1) * BLK].astype(F32) * inv[1]
            nsend[0, t, b, r, :] = jnp.where(swap, v1, v0).astype(BF16)
            nsend[1, t, b, r, :] = jnp.where(swap, v0, v1).astype(BF16)
        i0 = jnp.broadcast_to(inv[0], (16, 128))
        i1 = jnp.broadcast_to(inv[1], (16, 128))
        invs[0, r, :] = jnp.where(swap, i1, i0)
        invs[1, r, :] = jnp.where(swap, i0, i1)

    loop(0, SEQ // 16, norm_rows)

    n_back = jnp.where(back_up, 16, 0) - jnp.where(self_up, 1, 0) + jnp.where(even, 1, 0)
    pl.semaphore_wait(bar, 18 + n_back)

    low = pl.ds(0, HALF)
    high = pl.ds(HALF, HALF)

    def send_w(zz, part_rows, i, to):
        ref = wall.at[zz, part_rows]
        remote(ref, ref, w_s.at[i], w_r.at[i], dev(p, x, to, c)).start()

    load_kw.wait()
    load_vw.wait()
    send_w(zh, low, 0, zp)
    send_w(zh, high, 3, zm)
    send_w(zh, high, 1, zp)
    send_w(zh, low, 2, zm)
    for j, zz in ((1, zp), (2, zf), (3, zm)):
        remote(gall.at[zh], gall.at[zh], g_s.at[j], g_r.at[j], dev(p, x, zz, c)).start()

    def send_down(j):
        t = lax.rem(slot + j, 8)
        to = dev(p, lax.div(t, 2), zh, lax.rem(t, 2))
        remote(nsend.at[0, t], nrecv.at[0, slot], ns_s.at[0, t], ns_r.at[0, slot], to).start()

    loop(1, 8, send_down)
    own_norm = pltpu.make_async_copy(nsend.at[0, slot], nrecv.at[0, slot], lsem.at[5])
    own_norm.start()

    eye64 = lax.broadcasted_iota(jnp.int32, (SEQ, SEQ), 0) == lax.broadcasted_iota(
        jnp.int32, (SEQ, SEQ), 1
    )
    row_id = lax.broadcasted_iota(jnp.int32, (SEQ, SEQ), 0)
    col_id = lax.broadcasted_iota(jnp.int32, (SEQ, SEQ), 1)
    for m in range(2):
        start_row = (col_id - pos[m]).astype(F32)
        start_col = jnp.sum(jnp.where(eye64, start_row, 0.0), axis=1, keepdims=True)
        seen = jnp.logical_and(row_id >= col_id, start_row == start_col)
        vis[m] = jnp.where(seen, 1.0, 0.0)
    load_q.wait()
    load_og.wait()
    scale = HD ** (-0.5)

    def attend(i):
        m = lax.div(i, KVH)
        k = lax.rem(i, KVH)
        cols = pl.ds(pl.multiple_of(k * HD, HD), HD)
        heads = [
            pl.ds(pl.multiple_of(k * (GROUP * HD) + g * HD, HD), HD) for g in range(GROUP)
        ]
        kk = keys[m, :, cols]
        vv = values[m, :, cols]
        qs = jnp.concatenate([q[m, :, h] for h in heads], axis=0)
        gs = jnp.concatenate([og[m, :, h] for h in heads], axis=0)
        seen = jnp.concatenate([vis[m]] * GROUP, axis=0) > 0.5
        s = jnp.where(seen, dot(qs, kk, 1, 1) * scale, -1e30)
        w = jnp.exp(s - jnp.max(s, axis=1, keepdims=True))
        probs = w / jnp.sum(w, axis=1, keepdims=True)
        pb = probs.astype(BF16)
        attn = dot(pb, vv, 1, 0).astype(BF16)
        delta = jnp.sum(gs.astype(F32) * attn.astype(F32), axis=1, keepdims=True)
        ds = (probs * (dot(gs, vv, 1, 1) - delta)).astype(BF16)
        qgs = (dot(ds, kk, 1, 0) * scale).astype(BF16)
        for g, h in enumerate(heads):
            qg[m, :, h] = qgs[g * SEQ : (g + 1) * SEQ]
        kvm[m, :, cols] = (dot(ds, qs, 0, 0) * scale).astype(BF16)
        kvm[m, :, pl.ds(pl.multiple_of(KVW + k * HD, HD), HD)] = dot(pb, gs, 0, 0).astype(BF16)

    loop(0, 2 * KVH, attend)
    store_qg = pltpu.make_async_copy(qg, qg_hbm, lsem.at[6])
    store_qg.start()

    lane = lax.broadcasted_iota(jnp.int32, (SEQ, 128), 1)

    def split3(v):
        hi = v.astype(BF16).astype(F32)
        mid = (v - hi).astype(BF16).astype(F32)
        low = v - hi - mid
        return jnp.where(lane == 0, hi, jnp.where(lane == 1, mid, low)).astype(BF16)

    kv0 = kvm[0].astype(F32)
    kv1 = kvm[1].astype(F32)
    kvsnd[:, 0:KW] = jnp.where(swap, kv0, kv1).astype(BF16)
    kvsnd[:, KW:KX] = split3(invs[1])
    remote(kvsnd, kvall.at[1, slot], km_s.at[0], km_r.at[0], dev(7 - p, x, mir(c), c)).start()
    kvall[0, slot, :, 0:KW] = jnp.where(swap, kv1, kv0).astype(BF16)
    kvall[0, slot, :, KW:KX] = split3(invs[0])

    def spread_kv(e):
        mine = kvall.at[e, slot]
        for j in (1, 2, 3):
            xx = lax.rem(x + j, 4)
            remote(mine, mine, kx_s.at[e, j], kx_r.at[e, x], dev(p, xx, zh, c)).start()
        remote(mine, mine, kc_s.at[e, x], kc_r.at[e, x], dev(p, x, zh, 1 - c)).start()

    spread_kv(0)

    def send_up(j):
        t = lax.rem(slot + j, 8)
        to = dev(7 - p, lax.div(t, 2), mir(c), lax.rem(t, 2))
        remote(nsend.at[1, t], nrecv.at[1, slot], ns_s.at[1, t], ns_r.at[1, slot], to).start()

    loop(0, 8, send_up)

    here(km_s.at[0], km_r.at[0], kvall.at[1, slot]).wait_recv()
    spread_kv(1)
    def got_w(zz, part_rows, i):
        here(w_s.at[i], w_r.at[i], wall.at[zz, part_rows]).wait_recv()

    got_w(zm, low, 0)
    send_w(zm, low, 4, zp)
    got_w(zp, high, 3)
    send_w(zp, high, 5, zm)

    for e in range(2):
        for j in (1, 3, 2):
            xx = lax.rem(x + j, 4)
            got = kvall.at[e, xx * 2 + c]
            here(kx_s.at[e, j], kx_r.at[e, xx], got).wait_recv()
            remote(got, got, kc_s.at[e, xx], kc_r.at[e, xx], dev(p, x, zh, 1 - c)).start()

    own_norm.wait()

    def wait_norm(j):
        t = lax.rem(slot + j, 8)
        here(ns_s.at[1, t], ns_r.at[1, t], nrecv.at[1, t]).wait_recv()

        @pl.when(j > 0)
        def _():
            here(ns_s.at[0, t], ns_r.at[0, t], nrecv.at[0, t]).wait_recv()

    loop(0, 8, wait_norm)
    for e in range(2):
        for xx in range(4):
            here(kc_s.at[e, xx], kc_r.at[e, xx], kvall.at[e, xx * 2 + 1 - c]).wait_recv()
    for j, zz in ((1, zm), (2, zf), (3, zp)):
        here(g_s.at[j], g_r.at[j], gall.at[zz]).wait_recv()

    def weight_grad(b, store):
        g = gall[b, 0:1, :].astype(F32)
        for e in range(2):
            n = nrecv[e, :, b].reshape(8 * SEQ, BLK)
            hbuf[e * 8 * SEQ : (e + 1) * 8 * SEQ, :] = (n.astype(F32) * g).astype(BF16)

        def cols(i):
            cc = pl.ds(pl.multiple_of(i * BLK, BLK), BLK)
            kvc = kvall[:, :, :, cc].reshape(16 * SEQ, BLK)
            store(cc, dot(hbuf[...], kvc, 0, 0))

        loop(0, KW // BLK, cols)

    def send_rs(src, dst, i, to):
        remote(src, dst, rs_s.at[i], rs_r.at[i], dev(p, x, to, c)).start()

    def to_far(cc, v):
        rsf_s[:, cc] = v.astype(BF16)

    def to_next(cc, v):
        part[0, 0:MOST, cc] = v[0:MOST]
        rsn_s[0, MOST:BLK, cc] = v[MOST:BLK].astype(BF16)

    def to_prev(cc, v):
        part[1, 0:HALF, cc] = v[HALF:BLK]
        rsn_s[1, 0:HALF, cc] = v[0:HALF].astype(BF16)

    def to_own(cc, v):
        own[:, cc] = v

    third = pl.ds(HALF, HALF // 2)
    fourth = pl.ds(HALF + HALF // 2, HALF // 2)
    upward = lax.rem(p, 4) == 0
    weight_grad(zf, to_far)
    send_rs(rsf_s.at[low], rsf_r.at[low], 0, zp)
    send_rs(rsf_s.at[third], rsf_r.at[third], 1, jnp.where(upward, zp, zm))
    send_rs(rsf_s.at[fourth], rsf_r.at[fourth], 2, zm)
    weight_grad(zp, to_next)
    send_rs(rsn_s.at[0, fourth], rsn_r.at[0, fourth], 3, zp)
    weight_grad(zm, to_prev)
    send_rs(rsn_s.at[1, low], rsn_r.at[1, low], 4, zm)

    got_w(zm, high, 1)
    got_w(zp, low, 2)
    got_w(zf, low, 4)
    got_w(zf, high, 5)
    cacc[...] = jnp.zeros_like(cacc)
    eye = lax.broadcasted_iota(jnp.int32, (128, 128), 0) == lax.broadcasted_iota(
        jnp.int32, (128, 128), 1
    )

    def hidden_grad(e):
        def block(b):
            g = gall[b, 0:1, :].astype(F32)
            hg = dot(kvall[e, :, :, 0:KW].reshape(8 * SEQ, KW), wall[b], 1, 1)
            n = nrecv[e, :, b].reshape(8 * SEQ, BLK).astype(F32)
            gpart[e, b] = jnp.sum((hg * n).reshape(SEQ, 8, BLK), axis=0)
            ng = (hg * g).astype(BF16)
            ngb[e, :, b] = ng.reshape(8, SEQ, BLK)
            t = ng.astype(F32) * n
            cacc[e] = cacc[e] + t[:, 0:128] + t[:, 128:256]

        loop(0, 4, block)
        for i in range(4):
            col = jnp.sum(cacc[e, i * 128 : (i + 1) * 128, :], axis=1, keepdims=True)
            c_s[e, i : i + 1, :] = jnp.sum(jnp.where(eye, col, 0.0), axis=0, keepdims=True)
        c_r[e, slot] = c_s[e]

        def send_c(j):
            t = lax.rem(slot + j, 8)
            to = dev(p, lax.div(t, 2), zh, lax.rem(t, 2))
            remote(c_s.at[e], c_r.at[e, slot], c_ss.at[e, t], c_rs.at[e, slot], to).start()

        loop(1, 8, send_c)

    hidden_grad(1)
    hidden_grad(0)
    gsum[...] = gpart[0] + gpart[1]
    for j, zz in ((1, zp), (2, zf), (3, zm)):
        remote(gsum.at[zz], gg_r.at[j], gg_ss.at[j], gg_rs.at[j], dev(p, x, zz, c)).start()

    @pl.when(jnp.logical_not(back_down))
    def _():
        brecv[0] = jnp.zeros_like(brecv[0])

    @pl.when(jnp.logical_not(back_up))
    def _():
        brecv[1] = jnp.zeros_like(brecv[1])

    def branch(e):
        def wait_c(j):
            t = lax.rem(slot + j, 8)
            here(c_ss.at[e, t], c_rs.at[e, t], c_r.at[e, t]).wait_recv()

        loop(1, 8, wait_c)
        mean = jnp.sum(c_r[e], axis=0) * (1.0 / D)
        for i in range(4):
            col = jnp.sum(jnp.where(eye, mean[i : i + 1, :], 0.0), axis=1, keepdims=True)
            cbuf[e, 2 * i : 2 * i + 2] = jnp.broadcast_to(col, (128, 128)).reshape(2, SEQ, 128)

        def chunk(t):
            mc = cbuf[e, t][:, 0:1]
            parts3 = kvall[e, t, :, KW:KX].astype(F32)
            inv = jnp.sum(jnp.where(lane < 3, parts3, 0.0), axis=1, keepdims=True)
            for b in range(4):
                n = nrecv[e, t, b].astype(F32)
                bsend[e, t, b] = (inv * (ngb[e, t, b].astype(F32) - n * mc)).astype(BF16)

        loop(0, 8, chunk)

    branch(1)
    branch(0)

    def pass_on(j):
        t = lax.rem(slot - j + 8, 8)

        @pl.when(even)
        def _():
            here(u_s.at[t], u_r.at[t], relay.at[t]).wait_recv()
            remote(relay.at[t], brecv.at[1, t], u_s.at[t], b_r.at[1, t], dev(p + 1, x, zh, c)).start()

    def send_back(j):
        t = lax.rem(slot + j, 8)
        xx = lax.div(t, 2)
        cc = lax.rem(t, 2)
        is_self = jnp.logical_and(self_up, j == 0)

        @pl.when(odd)
        def _():
            to = dev(7 - p, xx, mir(cc), cc)
            remote(bsend.at[1, t], relay.at[slot], b_s.at[1, t], u_r.at[slot], to).start()

        @pl.when(jnp.logical_and(even_up, jnp.logical_not(is_self)))
        def _():
            to = dev(8 - p, xx, mir(cc), cc)
            remote(bsend.at[1, t], brecv.at[1, slot], b_s.at[1, t], b_r.at[1, slot], to).start()

        @pl.when(is_self)
        def _():
            pltpu.make_async_copy(bsend.at[1, t], brecv.at[1, slot], b_r.at[1, slot]).start()

        @pl.when(back_up)
        def _():
            to = dev(p - 1, xx, zh, cc)
            remote(bsend.at[0, t], brecv.at[0, slot], b_s.at[0, t], b_r.at[0, slot], to).start()

    loop(0, 8, send_back)

    here(rs_s.at[0], rs_r.at[0], rsf_r.at[low]).wait_recv()
    rsn_s[0, 0:HALF, :] = (part[0, 0:HALF, :] + rsf_r[0:HALF, :].astype(F32)).astype(BF16)
    send_rs(rsn_s.at[0, low], rsn_r.at[0, low], 5, zp)
    here(rs_s.at[1], rs_r.at[1], rsf_r.at[third]).wait_recv()
    more = rsf_r[HALF:MOST, :].astype(F32)
    rsn_s[0, HALF:MOST, :] = (part[0, HALF:MOST, :] + jnp.where(upward, more, 0.0)).astype(BF16)
    send_rs(rsn_s.at[0, third], rsn_r.at[0, third], 7, zp)
    rsn_s[1, HALF:MOST, :] = (part[1, 0 : MOST - HALF, :] + jnp.where(upward, 0.0, more)).astype(BF16)
    send_rs(rsn_s.at[1, third], rsn_r.at[1, third], 8, zm)
    here(rs_s.at[2], rs_r.at[2], rsf_r.at[fourth]).wait_recv()
    rsn_s[1, MOST:BLK, :] = (part[1, MOST - HALF : HALF, :] + rsf_r[MOST:BLK, :].astype(F32)).astype(BF16)
    send_rs(rsn_s.at[1, fourth], rsn_r.at[1, fourth], 6, zm)

    loop(0, 8, pass_on)

    weight_grad(zh, to_own)

    near = ((3, 0, fourth), (4, 1, low), (5, 0, low), (6, 1, fourth), (7, 0, third), (8, 1, third))
    for i, side, piece in near:
        here(rs_s.at[i], rs_r.at[i], rsn_r.at[side, piece]).wait_recv()
    wg = own[...] + rsn_r[0].astype(F32) + rsn_r[1].astype(F32)
    wk_out[...] = wg[:, 0:KVW]
    wv_out[...] = wg[:, KVW:KW]
    gg = gsum[zh]
    for j in (1, 2, 3):
        here(gg_ss.at[j], gg_rs.at[j], gg_r.at[j]).wait_recv()
        gg = gg + gg_r[j]
    gg_out[...] = jnp.sum(gg, axis=0, keepdims=True)

    def take_back(j):
        t = lax.rem(slot - j + 8, 8)

        @pl.when(back_down)
        def _():
            here(b_s.at[0, t], b_r.at[0, t], brecv.at[0, t]).wait_recv()

        @pl.when(back_up)
        def _():
            here(b_s.at[1, t], b_r.at[1, t], brecv.at[1, t]).wait_recv()

        for b in range(4):
            start = lax.div(t, 2) * (8 * BLK) + b * (2 * BLK) + lax.rem(t, 2) * BLK
            cols = pl.ds(pl.multiple_of(start, BLK), BLK)
            down = brecv[0, t, b].astype(F32)
            up = brecv[1, t, b].astype(F32)
            passed_out[0, :, cols] = jnp.where(swap, up, down).astype(BF16)
            passed_out[1, :, cols] = jnp.where(swap, down, up).astype(BF16)

    loop(0, 8, take_back)

    def drain(t):
        here(ns_s.at[1, t], ns_r.at[1, t], nsend.at[1, t]).wait_send()

        @pl.when(t != slot)
        def _():
            here(ns_s.at[0, t], ns_r.at[0, t], nsend.at[0, t]).wait_send()
            for e in range(2):
                here(c_ss.at[e, t], c_rs.at[e, t], c_s.at[e]).wait_send()

        @pl.when(even)
        def _():
            here(u_s.at[t], u_r.at[t], relay.at[t]).wait_send()

        @pl.when(back_up)
        def _():
            here(b_s.at[0, t], b_r.at[0, t], bsend.at[0, t]).wait_send()

        @pl.when(jnp.logical_and(back_up, jnp.logical_not(jnp.logical_and(self_up, t == slot))))
        def _():
            here(b_s.at[1, t], b_r.at[1, t], bsend.at[1, t]).wait_send()

    loop(0, 8, drain)
    here(km_s.at[0], km_r.at[0], kvsnd).wait_send()
    for e in range(2):
        for j in (1, 2, 3):
            here(kx_s.at[e, j], kx_r.at[e, j], kvall.at[e, slot]).wait_send()
        for xx in range(4):
            here(kc_s.at[e, xx], kc_r.at[e, xx], kvall.at[e, xx * 2 + c]).wait_send()
    for j in (1, 2, 3):
        here(g_s.at[j], g_r.at[j], gall.at[zh]).wait_send()
        here(gg_ss.at[j], gg_rs.at[j], gg_r.at[j]).wait_send()
    for i in range(6):
        here(w_s.at[i], w_r.at[i], wall.at[zh, low]).wait_send()
    for i, piece in ((0, low), (1, third), (2, fourth)):
        here(rs_s.at[i], rs_r.at[i], rsf_s.at[piece]).wait_send()
    for i, side, piece in near:
        here(rs_s.at[i], rs_r.at[i], rsn_s.at[side, piece]).wait_send()
    store_qg.wait()


def deliver(qg, passed, wk, wv, gg, qg_out, passed_out, wk_out, wv_out, gg_out, sem):
    copies = [
        pltpu.make_async_copy(wk, wk_out, sem.at[0]),
        pltpu.make_async_copy(wv, wv_out, sem.at[1]),
        pltpu.make_async_copy(gg, gg_out, sem.at[2]),
    ]
    for m in range(2):
        for h in range(2):
            rows = pl.ds(h * (SEQ // 2), SEQ // 2)
            i = 3 + 4 * m + 2 * h
            copies.append(
                pltpu.make_async_copy(passed.at[m, rows], passed_out.at[m, rows], sem.at[i])
            )
            copies.append(pltpu.make_async_copy(qg.at[m, rows], qg_out.at[m, rows], sem.at[i + 1]))
    for copy in copies:
        copy.start()
    for copy in copies:
        copy.wait()


def on_device(
    queries,
    keys,
    values,
    out_grad,
    block_input,
    positions,
    direction,
    key_weight,
    value_weight,
    gain,
):
    vmem = pl.BlockSpec(memory_space=pltpu.VMEM)
    smem = pl.BlockSpec(memory_space=pltpu.SMEM)
    hbm = pl.BlockSpec(memory_space=pl.ANY)
    dma = pltpu.SemaphoreType.DMA
    scratch = [
        pltpu.VMEM((2, SEQ, QW), BF16),
        pltpu.VMEM((2, SEQ, QW), BF16),
        pltpu.VMEM((2, SEQ, QW), BF16),
        pltpu.VMEM((2, SEQ, D), BF16),
        pltpu.VMEM((2, 8, 4, SEQ, BLK), BF16),
        pltpu.VMEM((2, 8, 4, SEQ, BLK), BF16),
        pltpu.VMEM((2, SEQ, 128), F32),
        pltpu.VMEM((2, SEQ, SEQ), F32),
        pltpu.VMEM((2, SEQ, KW), BF16),
        pltpu.VMEM((SEQ, KX), BF16),
        pltpu.VMEM((2, 8, SEQ, KX), BF16),
        pltpu.VMEM((4, BLK, KW), BF16),
        pltpu.VMEM((4, 16, BLK), BF16),
        pltpu.VMEM((16 * SEQ, BLK), BF16),
        pltpu.VMEM((2, MOST, KW), F32),
        pltpu.VMEM((BLK, KW), F32),
        pltpu.VMEM((BLK, KW), BF16),
        pltpu.VMEM((BLK, KW), BF16),
        pltpu.VMEM((2, BLK, KW), BF16),
        pltpu.VMEM((2, BLK, KW), BF16),
        pltpu.VMEM((2, 8, 4, SEQ, BLK), BF16),
        pltpu.VMEM((2, 8 * SEQ, 128), F32),
        pltpu.VMEM((2, 4, 8, BLK), F32),
        pltpu.VMEM((4, 8, BLK), F32),
        pltpu.VMEM((4, 8, BLK), F32),
        pltpu.VMEM((2, 8, 128), F32),
        pltpu.VMEM((2, 8, 8, 128), F32),
        pltpu.VMEM((2, 8, SEQ, 128), F32),
        pltpu.VMEM((2, 8, 4, SEQ, BLK), BF16),
        pltpu.VMEM((2, 8, 4, SEQ, BLK), BF16),
        pltpu.VMEM((8, 4, SEQ, BLK), BF16),
        dma((7,)),
        dma((2, 8)),
        dma((2, 8)),
        dma((4,)),
        dma((4,)),
        dma((1,)),
        dma((1,)),
        dma((2, 4)),
        dma((2, 4)),
        dma((2, 4)),
        dma((2, 4)),
        dma((6,)),
        dma((6,)),
        dma((9,)),
        dma((9,)),
        dma((4,)),
        dma((4,)),
        dma((2, 8)),
        dma((2, 8)),
        dma((2, 8)),
        dma((2, 8)),
        dma((8,)),
        dma((8,)),
    ]
    shapes = (
        jax.ShapeDtypeStruct((2, SEQ, QW), BF16),
        jax.ShapeDtypeStruct((2, SEQ, D), BF16),
        jax.ShapeDtypeStruct((BLK, KVW), F32),
        jax.ShapeDtypeStruct((BLK, KVW), F32),
        jax.ShapeDtypeStruct((1, BLK), F32),
    )
    results = pl.pallas_call(
        kernel,
        name="relay",
        out_shape=shapes,
        in_specs=[smem, vmem, vmem, vmem, vmem, hbm, hbm, hbm, hbm, hbm],
        out_specs=(hbm, vmem, vmem, vmem, vmem),
        scratch_shapes=scratch,
        compiler_params=pltpu.CompilerParams(
            collective_id=0, has_side_effects=True, vmem_limit_bytes=56 * 2**20
        ),
    )(
        direction,
        positions.reshape(2, 1, SEQ),
        keys[:, 0],
        values[:, 0],
        gain,
        queries[:, 0],
        out_grad[:, 0],
        block_input[:, 0],
        key_weight[0],
        value_weight[0],
    )
    qg, passed, wk, wv, gg = pl.pallas_call(
        deliver,
        name="deliver",
        out_shape=shapes,
        in_specs=[vmem] * 5,
        out_specs=(hbm,) * 5,
        scratch_shapes=[dma((11,))],
    )(*results)
    return qg[:, None], passed[:, None], wk[None], wv[None], gg


def solution(mesh):
    in_specs = (
        P(None, "pipe", "dp", None),
        P(None, "pipe", "dp", None),
        P(None, "pipe", "dp", None),
        P(None, "pipe", "dp", None),
        P(None, "pipe", "dp", None),
        P(None, "pipe", "dp"),
        P(),
        P("pipe", "dp", None),
        P("pipe", "dp", None),
        P("pipe", "dp"),
    )
    out_specs = (
        P(None, "pipe", "dp", None),
        P(None, "pipe", "dp", None),
        P("pipe", "dp", None),
        P("pipe", "dp", None),
        P("pipe", "dp"),
    )
    return jax.shard_map(
        on_device, mesh=mesh, in_specs=in_specs, out_specs=out_specs, check_vma=False
    )
```

```python
import functools

import jax
import jax.numpy as jnp
from jax import lax
from jax.experimental import pallas as pl
from jax.experimental.pallas import tpu as pltpu
from jax.sharding import PartitionSpec as P

KVH = 4
HD = 128
GROUP = 8
SEQ = 64
QW = 4096
KVW = 512
D = 8192
BLK = 256
KW = 2 * KVW
KX = KW + 128
HALF = BLK // 2
MOST = HALF + HALF // 2
MESH = pl.DeviceIdType.MESH
F32 = jnp.float32
BF16 = jnp.bfloat16


def dot(a, b, ca, cb):
    return lax.dot_general(a, b, (((ca,), (cb,)), ((), ())), preferred_element_type=F32)


def kernel(
    flag,
    pos,
    keys,
    values,
    gain,
    q_hbm,
    og_hbm,
    inp_hbm,
    kw_hbm,
    vw_hbm,
    qg_hbm,
    passed_out,
    wk_out,
    wv_out,
    gg_out,
    qg,
    q,
    og,
    inp,
    nsend,
    nrecv,
    invs,
    vis,
    kvm,
    kvsnd,
    kvall,
    wall,
    gall,
    hbuf,
    part,
    own,
    rsf_s,
    rsf_r,
    rsn_s,
    rsn_r,
    ngb,
    cacc,
    gpart,
    gsum,
    gg_r,
    c_s,
    c_r,
    cbuf,
    bsend,
    brecv,
    relay,
    lsem,
    ns_s,
    ns_r,
    g_s,
    g_r,
    km_s,
    km_r,
    kx_s,
    kx_r,
    kc_s,
    kc_r,
    w_s,
    w_r,
    rs_s,
    rs_r,
    gg_ss,
    gg_rs,
    c_ss,
    c_rs,
    b_s,
    b_r,
    u_s,
    u_r,
):
    p = lax.axis_index("pipe")
    d = lax.axis_index("dp")
    zl = lax.div(p, 4)
    x = lax.div(d, 8)
    zh = lax.rem(lax.div(d, 2), 4)
    c = lax.rem(d, 2)
    slot = x * 2 + c
    zp = lax.rem(zh + 1, 4)
    zf = lax.rem(zh + 2, 4)
    zm = lax.rem(zh + 3, 4)

    def dev(pp, xx, zz, cc):
        return (pp, xx * 8 + zz * 2 + cc)

    def mir(cc):
        return lax.rem(zh + 4 + cc * (2 * zl - 1), 4)

    def remote(src, dst, ss, rs, to):
        return pltpu.make_async_remote_copy(
            src_ref=src, dst_ref=dst, send_sem=ss, recv_sem=rs, device_id=to, device_id_type=MESH
        )

    def here(ss, rs, ref):
        return remote(ref, ref, ss, rs, dev(p, x, zh, 1 - c))

    def loop(lo, hi, f):
        def step(i, carry):
            f(i)
            return carry

        lax.fori_loop(lo, hi, step, 0)

    load_inp = pltpu.make_async_copy(inp_hbm, inp, lsem.at[0])
    load_kw = pltpu.make_async_copy(kw_hbm, wall.at[zh, :, pl.ds(0, KVW)], lsem.at[1])
    load_vw = pltpu.make_async_copy(vw_hbm, wall.at[zh, :, pl.ds(KVW, KVW)], lsem.at[2])
    load_q = pltpu.make_async_copy(q_hbm, q, lsem.at[3])
    load_og = pltpu.make_async_copy(og_hbm, og, lsem.at[4])
    load_kw.start()
    load_vw.start()
    load_inp.start()
    load_q.start()
    load_og.start()

    bar = pltpu.get_barrier_semaphore()

    def greet(to):
        pl.semaphore_signal(bar, inc=1, device_id=to, device_id_type=MESH)

    back_up = p >= 1
    back_down = p <= 6
    self_up = jnp.logical_and(p == 4, c == 0)
    zlm = lax.div(p + 3, 4) - 1
    zup = lax.rem(zh + 4 + c * (2 * zlm - 1), 4)

    even = lax.rem(p, 2) == 0
    odd = jnp.logical_not(even)
    even_up = jnp.logical_and(even, back_up)
    for zz in (zp, zm, zf):
        greet(dev(p, x, zz, c))

    @pl.when(odd)
    def _():
        greet(dev(p - 1, x, zh, c))

    def greet_all(j):
        t = lax.rem(slot + j, 8)
        xx = lax.div(t, 2)
        cc = lax.rem(t, 2)

        @pl.when(j > 0)
        def _():
            greet(dev(p, xx, zh, cc))

        greet(dev(7 - p, xx, mir(cc), cc))

        @pl.when(back_down)
        def _():
            greet(dev(p + 1, xx, zh, cc))

        @pl.when(even)
        def _():
            greet(dev(7 - p, xx, mir(c), cc))

        @pl.when(jnp.logical_and(even_up, jnp.logical_not(jnp.logical_and(self_up, j == 0))))
        def _():
            greet(dev(8 - p, xx, zup, cc))

    loop(0, 8, greet_all)
    gall[zh] = jnp.broadcast_to(gain[...], (16, BLK))

    swap = flag[0] == 1
    load_inp.wait()

    def norm_rows(i):
        r = pl.ds(pl.multiple_of(i * 16, 16), 16)
        sq = [jnp.zeros((16, BLK), F32), jnp.zeros((16, BLK), F32)]
        for j in range(32):
            for m in range(2):
                v = inp[m, r, j * BLK : (j + 1) * BLK].astype(F32)
                sq[m] = sq[m] + v * v
        inv = [lax.rsqrt(jnp.sum(s, axis=1, keepdims=True) * (1.0 / D) + 1e-05) for s in sq]
        for j in range(32):
            t = (j // 8) * 2 + j % 2
            b = (j // 2) % 4
            v0 = inp[0, r, j * BLK : (j + 1) * BLK].astype(F32) * inv[0]
            v1 = inp[1, r, j * BLK : (j + 1) * BLK].astype(F32) * inv[1]
            nsend[0, t, b, r, :] = jnp.where(swap, v1, v0).astype(BF16)
            nsend[1, t, b, r, :] = jnp.where(swap, v0, v1).astype(BF16)
        i0 = jnp.broadcast_to(inv[0], (16, 128))
        i1 = jnp.broadcast_to(inv[1], (16, 128))
        invs[0, r, :] = jnp.where(swap, i1, i0)
        invs[1, r, :] = jnp.where(swap, i0, i1)

    loop(0, SEQ // 16, norm_rows)

    n_back = jnp.where(back_up, 16, 0) - jnp.where(self_up, 1, 0) + jnp.where(even, 1, 0)
    pl.semaphore_wait(bar, 18 + n_back)

    low = pl.ds(0, HALF)
    high = pl.ds(HALF, HALF)

    def send_w(zz, part_rows, i, to):
        ref = wall.at[zz, part_rows]
        remote(ref, ref, w_s.at[i], w_r.at[i], dev(p, x, to, c)).start()

    load_kw.wait()
    load_vw.wait()
    send_w(zh, low, 0, zp)
    send_w(zh, high, 3, zm)
    send_w(zh, high, 1, zp)
    send_w(zh, low, 2, zm)
    for j, zz in ((1, zp), (2, zf), (3, zm)):
        remote(gall.at[zh], gall.at[zh], g_s.at[j], g_r.at[j], dev(p, x, zz, c)).start()

    def send_down(j):
        t = lax.rem(slot + j, 8)
        to = dev(p, lax.div(t, 2), zh, lax.rem(t, 2))
        remote(nsend.at[0, t], nrecv.at[0, slot], ns_s.at[0, t], ns_r.at[0, slot], to).start()

    loop(1, 8, send_down)
    own_norm = pltpu.make_async_copy(nsend.at[0, slot], nrecv.at[0, slot], lsem.at[5])
    own_norm.start()

    eye64 = lax.broadcasted_iota(jnp.int32, (SEQ, SEQ), 0) == lax.broadcasted_iota(
        jnp.int32, (SEQ, SEQ), 1
    )
    row_id = lax.broadcasted_iota(jnp.int32, (SEQ, SEQ), 0)
    col_id = lax.broadcasted_iota(jnp.int32, (SEQ, SEQ), 1)
    for m in range(2):
        start_row = (col_id - pos[m]).astype(F32)
        start_col = jnp.sum(jnp.where(eye64, start_row, 0.0), axis=1, keepdims=True)
        seen = jnp.logical_and(row_id >= col_id, start_row == start_col)
        vis[m] = jnp.where(seen, 1.0, 0.0)
    load_q.wait()
    load_og.wait()
    scale = HD ** (-0.5)

    def attend(i):
        m = lax.div(i, KVH)
        k = lax.rem(i, KVH)
        cols = pl.ds(pl.multiple_of(k * HD, HD), HD)
        heads = [
            pl.ds(pl.multiple_of(k * (GROUP * HD) + g * HD, HD), HD) for g in range(GROUP)
        ]
        kk = keys[m, :, cols]
        vv = values[m, :, cols]
        qs = jnp.concatenate([q[m, :, h] for h in heads], axis=0)
        gs = jnp.concatenate([og[m, :, h] for h in heads], axis=0)
        seen = jnp.concatenate([vis[m]] * GROUP, axis=0) > 0.5
        s = jnp.where(seen, dot(qs, kk, 1, 1) * scale, -1e30)
        w = jnp.exp(s - jnp.max(s, axis=1, keepdims=True))
        probs = w / jnp.sum(w, axis=1, keepdims=True)
        pb = probs.astype(BF16)
        attn = dot(pb, vv, 1, 0).astype(BF16)
        delta = jnp.sum(gs.astype(F32) * attn.astype(F32), axis=1, keepdims=True)
        ds = (probs * (dot(gs, vv, 1, 1) - delta)).astype(BF16)
        qgs = (dot(ds, kk, 1, 0) * scale).astype(BF16)
        for g, h in enumerate(heads):
            qg[m, :, h] = qgs[g * SEQ : (g + 1) * SEQ]
        kvm[m, :, cols] = (dot(ds, qs, 0, 0) * scale).astype(BF16)
        kvm[m, :, pl.ds(pl.multiple_of(KVW + k * HD, HD), HD)] = dot(pb, gs, 0, 0).astype(BF16)

    loop(0, 2 * KVH, attend)
    store_qg = pltpu.make_async_copy(qg, qg_hbm, lsem.at[6])
    store_qg.start()

    lane = lax.broadcasted_iota(jnp.int32, (SEQ, 128), 1)

    def split3(v):
        hi = v.astype(BF16).astype(F32)
        mid = (v - hi).astype(BF16).astype(F32)
        low = v - hi - mid
        return jnp.where(lane == 0, hi, jnp.where(lane == 1, mid, low)).astype(BF16)

    kv0 = kvm[0].astype(F32)
    kv1 = kvm[1].astype(F32)
    kvsnd[:, 0:KW] = jnp.where(swap, kv0, kv1).astype(BF16)
    kvsnd[:, KW:KX] = split3(invs[1])
    remote(kvsnd, kvall.at[1, slot], km_s.at[0], km_r.at[0], dev(7 - p, x, mir(c), c)).start()
    kvall[0, slot, :, 0:KW] = jnp.where(swap, kv1, kv0).astype(BF16)
    kvall[0, slot, :, KW:KX] = split3(invs[0])

    def spread_kv(e):
        mine = kvall.at[e, slot]
        for j in (1, 2, 3):
            xx = lax.rem(x + j, 4)
            remote(mine, mine, kx_s.at[e, j], kx_r.at[e, x], dev(p, xx, zh, c)).start()
        remote(mine, mine, kc_s.at[e, x], kc_r.at[e, x], dev(p, x, zh, 1 - c)).start()

    spread_kv(0)

    def send_up(j):
        t = lax.rem(slot + j, 8)
        to = dev(7 - p, lax.div(t, 2), mir(c), lax.rem(t, 2))
        remote(nsend.at[1, t], nrecv.at[1, slot], ns_s.at[1, t], ns_r.at[1, slot], to).start()

    loop(0, 8, send_up)

    here(km_s.at[0], km_r.at[0], kvall.at[1, slot]).wait_recv()
    spread_kv(1)
    def got_w(zz, part_rows, i):
        here(w_s.at[i], w_r.at[i], wall.at[zz, part_rows]).wait_recv()

    got_w(zm, low, 0)
    send_w(zm, low, 4, zp)
    got_w(zp, high, 3)
    send_w(zp, high, 5, zm)

    for e in range(2):
        for j in (1, 3, 2):
            xx = lax.rem(x + j, 4)
            got = kvall.at[e, xx * 2 + c]
            here(kx_s.at[e, j], kx_r.at[e, xx], got).wait_recv()
            remote(got, got, kc_s.at[e, xx], kc_r.at[e, xx], dev(p, x, zh, 1 - c)).start()

    own_norm.wait()

    def wait_norm(j):
        t = lax.rem(slot + j, 8)
        here(ns_s.at[1, t], ns_r.at[1, t], nrecv.at[1, t]).wait_recv()

        @pl.when(j > 0)
        def _():
            here(ns_s.at[0, t], ns_r.at[0, t], nrecv.at[0, t]).wait_recv()

    loop(0, 8, wait_norm)
    for e in range(2):
        for xx in range(4):
            here(kc_s.at[e, xx], kc_r.at[e, xx], kvall.at[e, xx * 2 + 1 - c]).wait_recv()
    for j, zz in ((1, zm), (2, zf), (3, zp)):
        here(g_s.at[j], g_r.at[j], gall.at[zz]).wait_recv()

    def weight_grad(b, store):
        g = gall[b, 0:1, :].astype(F32)
        for e in range(2):
            n = nrecv[e, :, b].reshape(8 * SEQ, BLK)
            hbuf[e * 8 * SEQ : (e + 1) * 8 * SEQ, :] = (n.astype(F32) * g).astype(BF16)

        def cols(i):
            cc = pl.ds(pl.multiple_of(i * BLK, BLK), BLK)
            kvc = kvall[:, :, :, cc].reshape(16 * SEQ, BLK)
            store(cc, dot(hbuf[...], kvc, 0, 0))

        loop(0, KW // BLK, cols)

    def send_rs(src, dst, i, to):
        remote(src, dst, rs_s.at[i], rs_r.at[i], dev(p, x, to, c)).start()

    def to_far(cc, v):
        rsf_s[:, cc] = v.astype(BF16)

    def to_next(cc, v):
        part[0, 0:MOST, cc] = v[0:MOST]
        rsn_s[0, MOST:BLK, cc] = v[MOST:BLK].astype(BF16)

    def to_prev(cc, v):
        part[1, 0:HALF, cc] = v[HALF:BLK]
        rsn_s[1, 0:HALF, cc] = v[0:HALF].astype(BF16)

    def to_own(cc, v):
        own[:, cc] = v

    third = pl.ds(HALF, HALF // 2)
    fourth = pl.ds(HALF + HALF // 2, HALF // 2)
    upward = lax.rem(p, 4) == 0
    weight_grad(zf, to_far)
    send_rs(rsf_s.at[low], rsf_r.at[low], 0, zp)
    send_rs(rsf_s.at[third], rsf_r.at[third], 1, jnp.where(upward, zp, zm))
    send_rs(rsf_s.at[fourth], rsf_r.at[fourth], 2, zm)
    weight_grad(zp, to_next)
    send_rs(rsn_s.at[0, fourth], rsn_r.at[0, fourth], 3, zp)
    weight_grad(zm, to_prev)
    send_rs(rsn_s.at[1, low], rsn_r.at[1, low], 4, zm)

    got_w(zm, high, 1)
    got_w(zp, low, 2)
    got_w(zf, low, 4)
    got_w(zf, high, 5)
    cacc[...] = jnp.zeros_like(cacc)
    eye = lax.broadcasted_iota(jnp.int32, (128, 128), 0) == lax.broadcasted_iota(
        jnp.int32, (128, 128), 1
    )

    def hidden_grad(e):
        def block(b):
            g = gall[b, 0:1, :].astype(F32)
            hg = dot(kvall[e, :, :, 0:KW].reshape(8 * SEQ, KW), wall[b], 1, 1)
            n = nrecv[e, :, b].reshape(8 * SEQ, BLK).astype(F32)
            gpart[e, b] = jnp.sum((hg * n).reshape(SEQ, 8, BLK), axis=0)
            ng = (hg * g).astype(BF16)
            ngb[e, :, b] = ng.reshape(8, SEQ, BLK)
            t = ng.astype(F32) * n
            cacc[e] = cacc[e] + t[:, 0:128] + t[:, 128:256]

        loop(0, 4, block)
        for i in range(4):
            col = jnp.sum(cacc[e, i * 128 : (i + 1) * 128, :], axis=1, keepdims=True)
            c_s[e, i : i + 1, :] = jnp.sum(jnp.where(eye, col, 0.0), axis=0, keepdims=True)
        c_r[e, slot] = c_s[e]

        def send_c(j):
            t = lax.rem(slot + j, 8)
            to = dev(p, lax.div(t, 2), zh, lax.rem(t, 2))
            remote(c_s.at[e], c_r.at[e, slot], c_ss.at[e, t], c_rs.at[e, slot], to).start()

        loop(1, 8, send_c)

    hidden_grad(1)
    hidden_grad(0)
    gsum[...] = gpart[0] + gpart[1]
    for j, zz in ((1, zp), (2, zf), (3, zm)):
        remote(gsum.at[zz], gg_r.at[j], gg_ss.at[j], gg_rs.at[j], dev(p, x, zz, c)).start()

    @pl.when(jnp.logical_not(back_down))
    def _():
        brecv[0] = jnp.zeros_like(brecv[0])

    @pl.when(jnp.logical_not(back_up))
    def _():
        brecv[1] = jnp.zeros_like(brecv[1])

    def branch(e):
        def wait_c(j):
            t = lax.rem(slot + j, 8)
            here(c_ss.at[e, t], c_rs.at[e, t], c_r.at[e, t]).wait_recv()

        loop(1, 8, wait_c)
        mean = jnp.sum(c_r[e], axis=0) * (1.0 / D)
        for i in range(4):
            col = jnp.sum(jnp.where(eye, mean[i : i + 1, :], 0.0), axis=1, keepdims=True)
            cbuf[e, 2 * i : 2 * i + 2] = jnp.broadcast_to(col, (128, 128)).reshape(2, SEQ, 128)

        def chunk(t):
            mc = cbuf[e, t][:, 0:1]
            parts3 = kvall[e, t, :, KW:KX].astype(F32)
            inv = jnp.sum(jnp.where(lane < 3, parts3, 0.0), axis=1, keepdims=True)
            for b in range(4):
                n = nrecv[e, t, b].astype(F32)
                bsend[e, t, b] = (inv * (ngb[e, t, b].astype(F32) - n * mc)).astype(BF16)

        loop(0, 8, chunk)

    branch(1)
    branch(0)

    def pass_on(j):
        t = lax.rem(slot - j + 8, 8)

        @pl.when(even)
        def _():
            here(u_s.at[t], u_r.at[t], relay.at[t]).wait_recv()
            remote(relay.at[t], brecv.at[1, t], u_s.at[t], b_r.at[1, t], dev(p + 1, x, zh, c)).start()

    def send_back(j):
        t = lax.rem(slot + j, 8)
        xx = lax.div(t, 2)
        cc = lax.rem(t, 2)
        is_self = jnp.logical_and(self_up, j == 0)

        @pl.when(odd)
        def _():
            to = dev(7 - p, xx, mir(cc), cc)
            remote(bsend.at[1, t], relay.at[slot], b_s.at[1, t], u_r.at[slot], to).start()

        @pl.when(jnp.logical_and(even_up, jnp.logical_not(is_self)))
        def _():
            to = dev(8 - p, xx, mir(cc), cc)
            remote(bsend.at[1, t], brecv.at[1, slot], b_s.at[1, t], b_r.at[1, slot], to).start()

        @pl.when(is_self)
        def _():
            pltpu.make_async_copy(bsend.at[1, t], brecv.at[1, slot], b_r.at[1, slot]).start()

        @pl.when(back_up)
        def _():
            to = dev(p - 1, xx, zh, cc)
            remote(bsend.at[0, t], brecv.at[0, slot], b_s.at[0, t], b_r.at[0, slot], to).start()

    loop(0, 8, send_back)

    here(rs_s.at[0], rs_r.at[0], rsf_r.at[low]).wait_recv()
    rsn_s[0, 0:HALF, :] = (part[0, 0:HALF, :] + rsf_r[0:HALF, :].astype(F32)).astype(BF16)
    send_rs(rsn_s.at[0, low], rsn_r.at[0, low], 5, zp)
    here(rs_s.at[1], rs_r.at[1], rsf_r.at[third]).wait_recv()
    more = rsf_r[HALF:MOST, :].astype(F32)
    rsn_s[0, HALF:MOST, :] = (part[0, HALF:MOST, :] + jnp.where(upward, more, 0.0)).astype(BF16)
    send_rs(rsn_s.at[0, third], rsn_r.at[0, third], 7, zp)
    rsn_s[1, HALF:MOST, :] = (part[1, 0 : MOST - HALF, :] + jnp.where(upward, 0.0, more)).astype(BF16)
    send_rs(rsn_s.at[1, third], rsn_r.at[1, third], 8, zm)
    here(rs_s.at[2], rs_r.at[2], rsf_r.at[fourth]).wait_recv()
    rsn_s[1, MOST:BLK, :] = (part[1, MOST - HALF : HALF, :] + rsf_r[MOST:BLK, :].astype(F32)).astype(BF16)
    send_rs(rsn_s.at[1, fourth], rsn_r.at[1, fourth], 6, zm)

    loop(0, 8, pass_on)

    weight_grad(zh, to_own)

    near = ((3, 0, fourth), (4, 1, low), (5, 0, low), (6, 1, fourth), (7, 0, third), (8, 1, third))
    for i, side, piece in near:
        here(rs_s.at[i], rs_r.at[i], rsn_r.at[side, piece]).wait_recv()
    wg = own[...] + rsn_r[0].astype(F32) + rsn_r[1].astype(F32)
    wk_out[...] = wg[:, 0:KVW]
    wv_out[...] = wg[:, KVW:KW]
    gg = gsum[zh]
    for j in (1, 2, 3):
        here(gg_ss.at[j], gg_rs.at[j], gg_r.at[j]).wait_recv()
        gg = gg + gg_r[j]
    gg_out[...] = jnp.sum(gg, axis=0, keepdims=True)

    def take_back(j):
        t = lax.rem(slot - j + 8, 8)

        @pl.when(back_down)
        def _():
            here(b_s.at[0, t], b_r.at[0, t], brecv.at[0, t]).wait_recv()

        @pl.when(back_up)
        def _():
            here(b_s.at[1, t], b_r.at[1, t], brecv.at[1, t]).wait_recv()

        for b in range(4):
            start = lax.div(t, 2) * (8 * BLK) + b * (2 * BLK) + lax.rem(t, 2) * BLK
            cols = pl.ds(pl.multiple_of(start, BLK), BLK)
            down = brecv[0, t, b].astype(F32)
            up = brecv[1, t, b].astype(F32)
            passed_out[0, :, cols] = jnp.where(swap, up, down).astype(BF16)
            passed_out[1, :, cols] = jnp.where(swap, down, up).astype(BF16)

    loop(0, 8, take_back)

    def drain(t):
        here(ns_s.at[1, t], ns_r.at[1, t], nsend.at[1, t]).wait_send()

        @pl.when(t != slot)
        def _():
            here(ns_s.at[0, t], ns_r.at[0, t], nsend.at[0, t]).wait_send()
            for e in range(2):
                here(c_ss.at[e, t], c_rs.at[e, t], c_s.at[e]).wait_send()

        @pl.when(even)
        def _():
            here(u_s.at[t], u_r.at[t], relay.at[t]).wait_send()

        @pl.when(back_up)
        def _():
            here(b_s.at[0, t], b_r.at[0, t], bsend.at[0, t]).wait_send()

        @pl.when(jnp.logical_and(back_up, jnp.logical_not(jnp.logical_and(self_up, t == slot))))
        def _():
            here(b_s.at[1, t], b_r.at[1, t], bsend.at[1, t]).wait_send()

    loop(0, 8, drain)
    here(km_s.at[0], km_r.at[0], kvsnd).wait_send()
    for e in range(2):
        for j in (1, 2, 3):
            here(kx_s.at[e, j], kx_r.at[e, j], kvall.at[e, slot]).wait_send()
        for xx in range(4):
            here(kc_s.at[e, xx], kc_r.at[e, xx], kvall.at[e, xx * 2 + c]).wait_send()
    for j in (1, 2, 3):
        here(g_s.at[j], g_r.at[j], gall.at[zh]).wait_send()
        here(gg_ss.at[j], gg_rs.at[j], gg_r.at[j]).wait_send()
    for i in range(6):
        here(w_s.at[i], w_r.at[i], wall.at[zh, low]).wait_send()
    for i, piece in ((0, low), (1, third), (2, fourth)):
        here(rs_s.at[i], rs_r.at[i], rsf_s.at[piece]).wait_send()
    for i, side, piece in near:
        here(rs_s.at[i], rs_r.at[i], rsn_s.at[side, piece]).wait_send()
    store_qg.wait()


def deliver(qg, passed, wk, wv, gg, qg_out, passed_out, wk_out, wv_out, gg_out, vq, vp, vk, vv, vg, take, give):
    moves = [(gg, vg, gg_out), (wk, vk, wk_out), (wv, vv, wv_out)]
    for m in range(2):
        moves.append((qg.at[m], vq.at[m], qg_out.at[m]))
        for h in range(2):
            rows = pl.ds(h * (SEQ // 2), SEQ // 2)
            moves.append((passed.at[m, rows], vp.at[m, rows], passed_out.at[m, rows]))
    loads = [pltpu.make_async_copy(a, v, take.at[i]) for i, (a, v, _) in enumerate(moves)]
    stores = [pltpu.make_async_copy(v, b, give.at[i]) for i, (_, v, b) in enumerate(moves)]
    for load in loads:
        load.start()
    for load, store in zip(loads, stores):
        load.wait()
        store.start()
    for store in stores:
        store.wait()


def on_device(
    queries,
    keys,
    values,
    out_grad,
    block_input,
    positions,
    direction,
    key_weight,
    value_weight,
    gain,
):
    vmem = pl.BlockSpec(memory_space=pltpu.VMEM)
    smem = pl.BlockSpec(memory_space=pltpu.SMEM)
    hbm = pl.BlockSpec(memory_space=pl.ANY)
    dma = pltpu.SemaphoreType.DMA
    scratch = [
        pltpu.VMEM((2, SEQ, QW), BF16),
        pltpu.VMEM((2, SEQ, QW), BF16),
        pltpu.VMEM((2, SEQ, QW), BF16),
        pltpu.VMEM((2, SEQ, D), BF16),
        pltpu.VMEM((2, 8, 4, SEQ, BLK), BF16),
        pltpu.VMEM((2, 8, 4, SEQ, BLK), BF16),
        pltpu.VMEM((2, SEQ, 128), F32),
        pltpu.VMEM((2, SEQ, SEQ), F32),
        pltpu.VMEM((2, SEQ, KW), BF16),
        pltpu.VMEM((SEQ, KX), BF16),
        pltpu.VMEM((2, 8, SEQ, KX), BF16),
        pltpu.VMEM((4, BLK, KW), BF16),
        pltpu.VMEM((4, 16, BLK), BF16),
        pltpu.VMEM((16 * SEQ, BLK), BF16),
        pltpu.VMEM((2, MOST, KW), F32),
        pltpu.VMEM((BLK, KW), F32),
        pltpu.VMEM((BLK, KW), BF16),
        pltpu.VMEM((BLK, KW), BF16),
        pltpu.VMEM((2, BLK, KW), BF16),
        pltpu.VMEM((2, BLK, KW), BF16),
        pltpu.VMEM((2, 8, 4, SEQ, BLK), BF16),
        pltpu.VMEM((2, 8 * SEQ, 128), F32),
        pltpu.VMEM((2, 4, 8, BLK), F32),
        pltpu.VMEM((4, 8, BLK), F32),
        pltpu.VMEM((4, 8, BLK), F32),
        pltpu.VMEM((2, 8, 128), F32),
        pltpu.VMEM((2, 8, 8, 128), F32),
        pltpu.VMEM((2, 8, SEQ, 128), F32),
        pltpu.VMEM((2, 8, 4, SEQ, BLK), BF16),
        pltpu.VMEM((2, 8, 4, SEQ, BLK), BF16),
        pltpu.VMEM((8, 4, SEQ, BLK), BF16),
        dma((7,)),
        dma((2, 8)),
        dma((2, 8)),
        dma((4,)),
        dma((4,)),
        dma((1,)),
        dma((1,)),
        dma((2, 4)),
        dma((2, 4)),
        dma((2, 4)),
        dma((2, 4)),
        dma((6,)),
        dma((6,)),
        dma((9,)),
        dma((9,)),
        dma((4,)),
        dma((4,)),
        dma((2, 8)),
        dma((2, 8)),
        dma((2, 8)),
        dma((2, 8)),
        dma((8,)),
        dma((8,)),
    ]
    shapes = (
        jax.ShapeDtypeStruct((2, SEQ, QW), BF16),
        jax.ShapeDtypeStruct((2, SEQ, D), BF16),
        jax.ShapeDtypeStruct((BLK, KVW), F32),
        jax.ShapeDtypeStruct((BLK, KVW), F32),
        jax.ShapeDtypeStruct((1, BLK), F32),
    )
    results = pl.pallas_call(
        kernel,
        name="relay",
        out_shape=shapes,
        in_specs=[smem, vmem, vmem, vmem, vmem, hbm, hbm, hbm, hbm, hbm],
        out_specs=(hbm, vmem, vmem, vmem, vmem),
        scratch_shapes=scratch,
        compiler_params=pltpu.CompilerParams(
            collective_id=0, has_side_effects=True, vmem_limit_bytes=56 * 2**20
        ),
    )(
        direction,
        positions.reshape(2, 1, SEQ),
        keys[:, 0],
        values[:, 0],
        gain,
        queries[:, 0],
        out_grad[:, 0],
        block_input[:, 0],
        key_weight[0],
        value_weight[0],
    )
    qg, passed, wk, wv, gg = pl.pallas_call(
        deliver,
        name="deliver",
        out_shape=shapes,
        in_specs=[hbm] * 5,
        out_specs=(hbm,) * 5,
        scratch_shapes=[pltpu.VMEM(t.shape, t.dtype) for t in shapes] + [dma((9,)), dma((9,))],
    )(*results)
    return qg[:, None], passed[:, None], wk[None], wv[None], gg


def solution(mesh):
    in_specs = (
        P(None, "pipe", "dp", None),
        P(None, "pipe", "dp", None),
        P(None, "pipe", "dp", None),
        P(None, "pipe", "dp", None),
        P(None, "pipe", "dp", None),
        P(None, "pipe", "dp"),
        P(),
        P("pipe", "dp", None),
        P("pipe", "dp", None),
        P("pipe", "dp"),
    )
    out_specs = (
        P(None, "pipe", "dp", None),
        P(None, "pipe", "dp", None),
        P("pipe", "dp", None),
        P("pipe", "dp", None),
        P("pipe", "dp"),
    )
    return jax.shard_map(
        on_device, mesh=mesh, in_specs=in_specs, out_specs=out_specs, check_vma=False
    )
```
